256 devices in a mesh: dp: 8 (over z), fsdp: 32 (over x, y, core).
Axes of the slice: x: 4, y: 4, z: 8, core: 2. Of those that a mesh axis runs over, the one named last changes fastest.
Arguments:
- replica_grads: bfloat16 [8, 2, 7168, 768], P('dp', None, 'fsdp'), may hold values from -600 to 600
- momentum: float32 [2, 7168, 768], P(None, 'fsdp'), may hold values from -18 to 18
- weights: float32 [2, 7168, 768], P(None, 'fsdp'), may hold values from -6 to 6
Outputs:
- new_momentum: float32 [2, 7168, 768], P(None, 'fsdp')
- update: float32 [2, 7168, 768], P(None, 'fsdp')
- new_weights: float32 [2, 7168, 768], P(None, 'fsdp')
The draws below stay inside these ranges and needn't reach their ends.
All inputs are finite; a program needn't handle non-finite values.
Results may differ from the reference program's by a relative error of at most 0.0003.
Values sent between devices are 32-bit elements; how exact they have to be, the bound alone decides.
A program may use at most 64 MiB of HBM per device.

```python
import math
import jax
import jax.numpy as jnp
from jax import lax

D = 7168
R = 768
LAYERS = 2
ITERS = 2
N_DP = 8


def draw_replica_grads(key, part):
    key = jax.random.fold_in(key, 11)
    row_key = jax.random.fold_in(key, 0)
    column_key = jax.random.fold_in(key, 1)
    noise_key = jax.random.fold_in(key, 2)
    left_key = jax.random.fold_in(key, 4)
    right_key = jax.random.fold_in(key, 5)
    position = jnp.arange(D, dtype=jnp.float32) / D
    row_scale = jnp.exp(math.log(3.0) * position[None, :] + math.log(10.0) * jax.random.uniform(row_key, (LAYERS, D), dtype=jnp.float32))
    column_scale = jnp.exp(math.log(1.5) * jax.random.uniform(column_key, (LAYERS, R), dtype=jnp.float32))
    left_factors = jnp.clip(jax.random.normal(left_key, (LAYERS, D, 4), dtype=jnp.float32), -3.0, 3.0)
    right_factors = jnp.clip(jax.random.normal(right_key, (LAYERS, R, 4), dtype=jnp.float32), -3.0, 3.0)
    low_rank = left_factors[:, :, None, 0] * right_factors[:, None, :, 0]
    for factor_index in range(1, 4):
        low_rank = low_rank + left_factors[:, :, None, factor_index] * right_factors[:, None, :, factor_index]
    shared_weight = 0.5 / math.sqrt(N_DP)
    noise_part = jnp.clip(jax.random.normal(noise_key, (N_DP, LAYERS, D, R), dtype=jnp.float32), -4.0, 4.0)
    values = noise_part + shared_weight * low_rank[None]
    scaled = 0.05 * values * row_scale[None, :, :, None] * column_scale[None, :, None, :]
    return scaled.astype(jnp.bfloat16)


def block_levels(own_key, dims, cuts, low, top_value):
    def one(dim, shards_of):
        heights = jax.random.uniform(jax.random.fold_in(jax.random.fold_in(own_key, 6), dim), (shards_of,), jnp.float32, low / len(cuts), top_value / len(cuts))
        return jnp.repeat(jnp.exp(heights), dims[dim] // shards_of).reshape((-1,) + (1,) * (len(dims) - dim - 1))

    factor_of = one(*cuts[0])
    for cut in cuts[1:]:
        factor_of = factor_of * one(*cut)
    return factor_of


def bell_draw(own_key, extent, scale, bound, shards=(), kind=jnp.bfloat16):
    array = scale * jax.random.normal(own_key, extent, jnp.float32)
    if shards:
        array = array * block_levels(own_key, extent, shards, -0.22, 0.18)
    return jnp.clip(array, -bound, bound).astype(kind)


def setup_inputs(seed: int = 0) -> dict:
    key_list = jax.random.split(jax.random.key(seed), 4)
    replica_grads = draw_replica_grads(jax.random.fold_in(key_list[3], 71), 0)
    momentum = bell_draw(key_list[1], (LAYERS, D, R), 3.0, 18.0, ((1, 32),), jnp.float32)
    weights = bell_draw(key_list[2], (LAYERS, D, R), 1.0, 6.0, ((1, 32),), jnp.float32)
    return dict(replica_grads=replica_grads, momentum=momentum, weights=weights)


QUINTIC_LINEAR = 3.4445
QUINTIC_CUBIC = -4.775
QUINTIC_FIFTH = 2.0315
MOMENTUM_FACTOR = 0.95
LEARNING_RATE = 0.02
WEIGHT_DECAY = 0.1
NORM_EPSILON = 1e-07
UPDATE_FACTOR = 0.2

def orthogonalize(direction):
    squares_sum = jnp.sum(direction * direction)
    inverse_norm = 1.0 / (jnp.sqrt(squares_sum) + NORM_EPSILON)
    current = direction
    for iteration in range(ITERS):
        gram_matrix = jnp.dot(current.T, current, preferred_element_type=jnp.float32, precision=lax.Precision.HIGHEST)
        if iteration == 0:
            gram_matrix = gram_matrix * (inverse_norm * inverse_norm)
        product = jnp.dot(current, gram_matrix, preferred_element_type=jnp.float32, precision=lax.Precision.HIGHEST)
        second = jnp.dot(product, gram_matrix, preferred_element_type=jnp.float32, precision=lax.Precision.HIGHEST)
        current = QUINTIC_LINEAR * current + QUINTIC_CUBIC * product + QUINTIC_FIFTH * second
        if iteration == 0:
            current = current * inverse_norm
    return current

def reference(replica_grads, momentum, weights):
    summed = lax.optimization_barrier(jnp.sum(replica_grads.astype(jnp.float32), axis=0))
    new_momentum = MOMENTUM_FACTOR * momentum + summed
    direction = summed + MOMENTUM_FACTOR * new_momentum
    orthogonal = jnp.stack([orthogonalize(direction[layer_index]) for layer_index in range(LAYERS)])
    update = UPDATE_FACTOR * math.sqrt(max(D, R)) * orthogonal
    new_weights = weights - LEARNING_RATE * (update + WEIGHT_DECAY * weights)
    return (new_momentum, update, new_weights)
```

```python
import functools
import math

import jax
import jax.numpy as jnp
from jax import lax
from jax.experimental import pallas as pl
from jax.experimental.pallas import tpu as pltpu
from jax.sharding import PartitionSpec as P

D = 7168
R = 768

QUINTIC_LINEAR = 3.4445
QUINTIC_CUBIC = -4.775
QUINTIC_FIFTH = 2.0315
MOMENTUM_FACTOR = 0.95
LEARNING_RATE = 0.02
WEIGHT_DECAY = 0.1
NORM_EPSILON = 1e-07
UPDATE_FACTOR = 0.2

MESH = pl.DeviceIdType.MESH
F32 = jnp.float32
BF16 = jnp.bfloat16
NZ = 8
CH = 56
SUB = 3
W = R // SUB
BA, BB = 48, 40
BLOCKS = 11
SPLIT = 16 * BA


def device(x, y, z, c):
    return (z, (x * 4 + y) * 2 + c)


def remote(src, dst, send, recv, target):
    return pltpu.make_async_remote_copy(
        src_ref=src, dst_ref=dst, send_sem=send, recv_sem=recv, device_id=target, device_id_type=MESH
    )


def gram_kernel(
    g_ref, m_ref, s_ref, ga, gb,
    acc, rl, rs, mbuf, dx, dh, dl, packed, ra1, rb1, ra2, rb2, share, rz, piece, gz,
    msem, ls, lr, ss, sr, als, alr, ass, asr, cs, cr,
    a1s, a1r, b1s, b1r, a2s, a2r, b2s, b2r, z1s, z1r, z2s, z2r,
    ga1s, ga1r, gb1s, gb1r, ga2s, ga2r, gb2s, gb2r, gcs, gcr,
):
    z = lax.axis_index("dp")
    f = lax.axis_index("fsdp")
    c = f % 2
    y = (f // 2) % 4
    x = f // 8
    layer = z // 4
    q = z % 4
    other = device(x, y, z, 1 - c)
    way = 1 - 2 * c
    up = device(x, y, (z + way + NZ) % NZ, c)
    down = device(x, y, (z - way + NZ) % NZ, c)

    def chunk(offset):
        return (z + way * offset + 2 * NZ) % NZ

    fetch = pltpu.make_async_copy(m_ref.at[pl.ds(pl.multiple_of(z * CH, 8), CH)], mbuf, msem)
    fetch.start()

    barrier = pltpu.get_barrier_semaphore()
    greeted = [other]
    greeted += [device(x, y, (z + o) % NZ, c) for o in range(1, NZ)]
    greeted += [device((x + o) % 4, y, z, c) for o in range(1, 4)]
    greeted += [device(x, (y + o) % 4, z, c) for o in range(1, 4)]
    for target in greeted:
        pl.semaphore_signal(barrier, inc=1, device_id=target, device_id_type=MESH)
    for i in range(4):
        rows = g_ref[i * 2 * CH : (i + 1) * 2 * CH, :].astype(F32)
        acc[2 * i] = rows[:CH]
        acc[2 * i + 1] = rows[CH:]
    pl.semaphore_wait(barrier, len(greeted))

    def cols(k):
        return pl.ds(k * W, W)

    started = []

    def go(copy):
        copy.start()
        started.append(copy)
        return copy

    def long_hop(step, k):
        return remote(acc.at[chunk(4 - step), :, cols(k)], rl.at[step, :, cols(k)], ls.at[step, k], lr.at[step, k], up)

    def short_hop(step, k):
        return remote(acc.at[chunk(step - 3), :, cols(k)], rs.at[step, :, cols(k)], ss.at[step, k], sr.at[step, k], down)

    hops = {}
    for k in range(SUB):
        hops["l", 0, k] = go(long_hop(0, k))
        hops["s", 0, k] = go(short_hop(0, k))
    for step in range(1, 4):
        for k in range(SUB):
            hops["l", step - 1, k].wait_recv()
            at = chunk(4 - step)
            acc[at, :, cols(k)] = acc[at, :, cols(k)] + rl[step - 1, :, cols(k)]
            hops["l", step, k] = go(long_hop(step, k))
            if step < 3:
                hops["s", step - 1, k].wait_recv()
                at = chunk(step - 3)
                acc[at, :, cols(k)] = acc[at, :, cols(k)] + rs[step - 1, :, cols(k)]
                hops["s", step, k] = go(short_hop(step, k))

    def gather_up(step, k):
        at = chunk(-step)
        return remote(s_ref.at[at, :, cols(k)], s_ref.at[at, :, cols(k)], als.at[step, k], alr.at[step, k], up)

    def gather_down(step, k):
        at = chunk(step)
        return remote(s_ref.at[at, :, cols(k)], s_ref.at[at, :, cols(k)], ass.at[step, k], asr.at[step, k], down)

    fetch.wait()
    mine = []
    for k in range(SUB):
        hops["s", 2, k].wait_recv()
        hops["l", 3, k].wait_recv()
        total = acc[z, :, cols(k)] + rs[2, :, cols(k)] + rl[3, :, cols(k)]
        s_ref[z, :, cols(k)] = total
        d = total + MOMENTUM_FACTOR * (MOMENTUM_FACTOR * mbuf[:, cols(k)] + total)
        dx[0:CH, cols(k)] = d
        mine.append(
            go(remote(dx.at[pl.ds(0, CH), cols(k)], dx.at[pl.ds(CH, CH), cols(k)], cs.at[k], cr.at[k], other))
        )
        hops["u", 0, k] = go(gather_up(0, k))
        hops["d", 0, k] = go(gather_down(0, k))

    for k in range(SUB):
        mine[k].wait_recv()
        d = dx[:, cols(k)]
        hi = d.astype(BF16)
        lo = (d - hi.astype(F32)).astype(BF16)
        dh[:, cols(k)] = hi
        dl[:, cols(k)] = lo
        if k == 0:
            dh[:, R : R + W] = hi
            dl[:, R : R + W] = lo

    def gram(first, second, width):
        li = pl.ds(pl.multiple_of(first * 128, 128), 128)
        ri = pl.ds(pl.multiple_of(second * 128, 128), width)

        def dot(left, right):
            return lax.dot_general(left, right, (((0,), (0,)), ((), ())), preferred_element_type=F32)

        lh, ll, rh, rlo = dh[:, li], dl[:, li], dh[:, ri], dl[:, ri]
        return dot(lh, rh) + (dot(lh, rlo) + dot(ll, rh))

    for a in range(3):
        block = gram(3 * c + a, 3 * c + a, 384)
        for k in range(3):
            packed[(3 * a + k) * 128 : (3 * a + k + 1) * 128, :] = block[:, k * 128 : (k + 1) * 128]
    for b in range(2):
        packed[(9 + b) * 128 : (10 + b) * 128, :] = gram(2 * c + b, 2 * c + b + 3, 128)

    pa = (x * (1 - c) + y * c, y * (1 - c) + x * c)
    pb = (pa[1], pa[0])

    def on_a(first, second):
        return device(first * (1 - c) + second * c, second * (1 - c) + first * c, z, c)

    def on_b(first, second):
        return on_a(second, first)

    paths = (
        (0, BA, pa, on_a, ra1, ra2, a1s, a1r, a2s, a2r, ga, ga1s, ga1r, ga2s, ga2r),
        (SPLIT, BB, pb, on_b, rb1, rb2, b1s, b1r, b2s, b2r, gb, gb1s, gb1r, gb2s, gb2r),
    )
    order = (2, 1, 3)

    first_hops = []
    for base, rows, (p1, p2), on, r1, r2, s1, t1, s2, t2, *_ in paths:
        size = 4 * rows
        for o in order:
            to = (p1 + o) % 4
            src = packed.at[pl.ds(pl.multiple_of(base + to * size, 8), size)]
            first_hops.append(go(remote(src, r1.at[o - 1], s1.at[o - 1], t1.at[o - 1], on(to, p2))))

    for k in range(SUB):
        hops["u", 0, k].wait_recv()
        hops["u", 1, k] = go(gather_up(1, k))
        hops["d", 0, k].wait_recv()
        hops["d", 1, k] = go(gather_down(1, k))

    second_hops = []
    for n, (base, rows, (p1, p2), on, r1, r2, s1, t1, s2, t2, *_) in enumerate(paths):
        size = 4 * rows
        for hop in first_hops[3 * n : 3 * n + 3]:
            hop.wait_recv()
        own = pl.ds(pl.multiple_of(base + p1 * size, 8), size)
        r1[3] = (packed[own, :] + r1[0]) + (r1[1] + r1[2])
        for o in order:
            to = (p2 + o) % 4
            src = r1.at[3, pl.ds(pl.multiple_of(to * rows, 8), rows)]
            second_hops.append(go(remote(src, r2.at[o - 1], s2.at[o - 1], t2.at[o - 1], on(p1, to))))
    for n, (base, rows, (p1, p2), on, r1, r2, *_) in enumerate(paths):
        for hop in second_hops[3 * n : 3 * n + 3]:
            hop.wait_recv()
        own = pl.ds(pl.multiple_of(p2 * rows, 8), rows)
        start = 0 if n == 0 else BA
        share[start : start + rows, :] = (r1[3, own, :] + r2[0]) + (r2[1] + r2[2])
    share[BA + BB : 96, :] = jnp.zeros((96 - BA - BB, 128), F32)

    quarter = []
    for o in (2, 1, 3):
        to = (q + o) % 4
        src = share.at[pl.ds(pl.multiple_of(to * 24, 8), 24)]
        quarter.append(go(remote(src, rz.at[o - 1], z1s.at[o - 1], z1r.at[o - 1], device(x, y, layer * 4 + to, c))))
    for hop in quarter:
        hop.wait_recv()
    at = pl.ds(pl.multiple_of(q * 24, 8), 24)
    total = (share[at, :] + rz[0]) + (rz[1] + rz[2])
    piece[...] = total
    gz[layer, at, :] = total
    spread = []
    for o in (4, 3, 5, 2, 6, 1, 7):
        spread.append(
            go(remote(piece, gz.at[layer, at], z2s.at[o - 1], z2r.at[o - 1], device(x, y, (z + o) % NZ, c)))
        )
    for hop in spread:
        hop.wait_recv()

    near, far = [], []
    for n, (base, rows, (p1, p2), on, r1, r2, s1, t1, s2, t2, out, u1, v1, u2, v2) in enumerate(paths):
        start = 0 if n == 0 else BA
        out[c, p1, p2] = gz[:, start : start + rows, :]
        block = out.at[c, p1, p2]
        for o in order:
            near.append(go(remote(block, block, u1.at[o - 1], v1.at[o - 1], on(p1, (p2 + o) % 4))))
        for o in order:
            far.append(go(remote(block, block, u2.at[o - 1, 0], v2.at[o - 1, 0], on((p1 + o) % 4, p2))))

    for k in range(SUB):
        hops["u", 1, k].wait_recv()
        hops["u", 2, k] = go(gather_up(2, k))
        hops["d", 1, k].wait_recv()
        hops["d", 2, k] = go(gather_down(2, k))

    for i, o in enumerate(order):
        for n, (base, rows, (p1, p2), on, r1, r2, s1, t1, s2, t2, out, u1, v1, u2, v2) in enumerate(paths):
            near[3 * n + i].wait_recv()
            block = out.at[c, p1, (p2 + 4 - o) % 4]
            for e in order:
                far.append(go(remote(block, block, u2.at[e - 1, o], v2.at[e - 1, o], on((p1 + e) % 4, p2))))

    for k in range(SUB):
        hops["u", 2, k].wait_recv()
        hops["u", 3, k] = go(gather_up(3, k))

    crossing = []
    for n, (base, rows, (p1, p2), on, r1, r2, s1, t1, s2, t2, out, *_) in enumerate(paths):
        block = out.at[c, p1]
        crossing.append(go(remote(block, block, gcs.at[n, 0], gcr.at[n, 0], other)))
    for i, o in enumerate(order):
        for n, (base, rows, (p1, p2), on, r1, r2, s1, t1, s2, t2, out, *_) in enumerate(paths):
            far[3 * n + i].wait_recv()
            for j in range(3):
                far[6 + 6 * j + 3 * n + i].wait_recv()
            block = out.at[c, (p1 + 4 - o) % 4]
            crossing.append(go(remote(block, block, gcs.at[n, o], gcr.at[n, o], other)))
    for hop in crossing:
        hop.wait_recv()
    for k in range(SUB):
        hops["d", 2, k].wait_recv()
        hops["u", 3, k].wait_recv()
    for copy in started:
        copy.wait_send()


def split(value):
    hi = value.astype(BF16)
    return hi, (value - hi.astype(F32)).astype(BF16)


def dot3(left, right):
    (lh, ll), (rh, rl) = left, right

    def dot(a, b):
        return jnp.dot(a, b, preferred_element_type=F32)

    return dot(lh, rh) + (dot(lh, rl) + dot(ll, rh))


def symmetric_product(out, lh, ll, rh, rl):
    for j in range(3):
        rows = slice(0, (j + 1) * 256)
        at = slice(j * 256, (j + 1) * 256)
        block = dot3((lh[rows, :], ll[rows, :]), (rh[:, at], rl[:, at]))
        out[rows, at] = block
        for i in range(j):
            out[at, i * 256 : (i + 1) * 256] = block[i * 256 : (i + 1) * 256].T


def update_kernel(s_ref, m_ref, w_ref, ga, gb, nm_ref, up_ref, nw_ref, g, a2, ah, al, ph, plo, bh, bl):
    for layer in range(2):
        trace = jnp.zeros((), F32)
        eye = lax.broadcasted_iota(jnp.int32, (128, 128), 0) == lax.broadcasted_iota(jnp.int32, (128, 128), 1)
        for h in range(2):
            rows_a = ga[h, :, layer * BA : (layer + 1) * BA, :].reshape(16 * BA, 128)
            rows_b = gb[h, :, layer * BB : (layer + 1) * BB, :].reshape(16 * BB, 128)
            for b in range(BLOCKS):
                if b < 9:
                    i = 3 * h + b // 3
                    j = (i + b % 3) % 6
                else:
                    i = 2 * h + b - 9
                    j = (i + 3) % 6
                if i == 3:
                    if j == 0:
                        continue
                block = rows_a[b * 128 : (b + 1) * 128] if b < 6 else rows_b[(b - 6) * 128 : (b - 5) * 128]
                g[i * 128 : (i + 1) * 128, j * 128 : (j + 1) * 128] = block
                if i == j:
                    trace = trace + jnp.sum(jnp.where(eye, block, 0.0))
                else:
                    g[j * 128 : (j + 1) * 128, i * 128 : (i + 1) * 128] = block.T
        inverse = 1.0 / (jnp.sqrt(jnp.broadcast_to(trace, (8, 128))) + NORM_EPSILON)
        scale = inverse[0:1, 0:1]
        a = g[...] * (scale * scale)
        g[...] = a
        ah[...], al[...] = split(a)
        symmetric_product(a2, ah, al, ah, al)
        diagonal = lax.broadcasted_iota(jnp.int32, (R, R), 0) == lax.broadcasted_iota(jnp.int32, (R, R), 1)
        p = jnp.where(diagonal, QUINTIC_LINEAR, 0.0) + QUINTIC_CUBIC * g[...] + QUINTIC_FIFTH * a2[...]
        ph[...], plo[...] = split(p)
        symmetric_product(a2, ph, plo, ah, al)
        bh[...], bl[...] = split(a2[...])
        symmetric_product(g, ph, plo, bh, bl)
        ah[...], al[...] = split(g[...])
        rows = slice(layer * 224, (layer + 1) * 224)
        summed = s_ref[rows, :]
        new_momentum = MOMENTUM_FACTOR * m_ref[rows, :] + summed
        nm_ref[rows, :] = new_momentum
        direction = summed + MOMENTUM_FACTOR * new_momentum
        x1 = dot3(split(direction), (ph[...], plo[...])) * scale
        second = (ah[...], al[...])
        y = dot3(split(x1), second)
        t = dot3(split(y), second)
        orthogonal = QUINTIC_LINEAR * x1 + QUINTIC_CUBIC * y + QUINTIC_FIFTH * t
        update = UPDATE_FACTOR * math.sqrt(max(D, R)) * orthogonal
        up_ref[rows, :] = update
        weights = w_ref[rows, :]
        nw_ref[rows, :] = weights - LEARNING_RATE * (update + WEIGHT_DECAY * weights)


def shards(replica_grads, momentum, weights):
    grads = replica_grads.reshape(NZ * CH, R)
    momentum = momentum.reshape(NZ * CH, R)
    weights = weights.reshape(NZ * CH, R)
    vmem = pl.BlockSpec(memory_space=pltpu.VMEM)
    sem = pltpu.SemaphoreType.DMA
    summed, ga, gb = pl.pallas_call(
        gram_kernel,
        out_shape=(
            jax.ShapeDtypeStruct((NZ, CH, R), F32),
            jax.ShapeDtypeStruct((2, 4, 4, 2, BA, 128), F32),
            jax.ShapeDtypeStruct((2, 4, 4, 2, BB, 128), F32),
        ),
        in_specs=[vmem, pl.BlockSpec(memory_space=pl.ANY)],
        out_specs=(vmem, vmem, vmem),
        scratch_shapes=[
            pltpu.VMEM((NZ, CH, R), F32),
            pltpu.VMEM((4, CH, R), F32),
            pltpu.VMEM((3, CH, R), F32),
            pltpu.VMEM((CH, R), F32),
            pltpu.VMEM((2 * CH, R), F32),
            pltpu.VMEM((2 * CH, R + W), BF16),
            pltpu.VMEM((2 * CH, R + W), BF16),
            pltpu.VMEM((BLOCKS * 128, 128), F32),
            pltpu.VMEM((4, 4 * BA, 128), F32),
            pltpu.VMEM((4, 4 * BB, 128), F32),
            pltpu.VMEM((3, BA, 128), F32),
            pltpu.VMEM((3, BB, 128), F32),
            pltpu.VMEM((96, 128), F32),
            pltpu.VMEM((3, 24, 128), F32),
            pltpu.VMEM((24, 128), F32),
            pltpu.VMEM((2, 96, 128), F32),
            sem,
        ]
        + [sem((4, SUB)), sem((4, SUB)), sem((3, SUB)), sem((3, SUB))] * 2
        + [sem((SUB,))] * 2
        + [sem((3,))] * 10
        + [sem((7,))] * 2
        + [sem((3,))] * 4
        + [sem((3, 4))] * 4
        + [sem((2, 4))] * 2,
        compiler_params=pltpu.CompilerParams(collective_id=0, has_side_effects=True, vmem_limit_bytes=32 << 20),
        name="gram",
    )(grads, momentum)
    summed = summed.reshape(NZ * CH, R)
    ga = ga.reshape(2, 16, 2 * BA, 128)
    gb = gb.reshape(2, 16, 2 * BB, 128)
    like = jax.ShapeDtypeStruct((NZ * CH, R), F32)
    outs = pl.pallas_call(
        update_kernel,
        out_shape=(like, like, like),
        in_specs=[vmem] * 5,
        out_specs=(vmem, vmem, vmem),
        scratch_shapes=[pltpu.VMEM((R, R), F32)] * 2 + [pltpu.VMEM((R, R), BF16)] * 6,
        compiler_params=pltpu.CompilerParams(vmem_limit_bytes=48 << 20),
        name="update",
    )(summed, momentum, weights, ga, gb)
    return tuple(o.reshape(2, 224, R) for o in outs)


def solution(mesh):
    return jax.shard_map(
        shards,
        mesh=mesh,
        in_specs=(P("dp", None, "fsdp", None), P(None, "fsdp", None), P(None, "fsdp", None)),
        out_specs=(P(None, "fsdp", None), P(None, "fsdp", None), P(None, "fsdp", None)),
        check_vma=False,
    )
```

```python
import functools
import math

import jax
import jax.numpy as jnp
from jax import lax
from jax.experimental import pallas as pl
from jax.experimental.pallas import tpu as pltpu
from jax.sharding import PartitionSpec as P

D = 7168
R = 768

QUINTIC_LINEAR = 3.4445
QUINTIC_CUBIC = -4.775
QUINTIC_FIFTH = 2.0315
MOMENTUM_FACTOR = 0.95
LEARNING_RATE = 0.02
WEIGHT_DECAY = 0.1
NORM_EPSILON = 1e-07
UPDATE_FACTOR = 0.2

MESH = pl.DeviceIdType.MESH
F32 = jnp.float32
BF16 = jnp.bfloat16
NZ = 8
CH = 56
SUB = 3
W = R // SUB
BA, BB = 48, 40
BLOCKS = 11
SPLIT = 16 * BA


def device(x, y, z, c):
    return (z, (x * 4 + y) * 2 + c)


def remote(src, dst, send, recv, target):
    return pltpu.make_async_remote_copy(
        src_ref=src, dst_ref=dst, send_sem=send, recv_sem=recv, device_id=target, device_id_type=MESH
    )


def gram_kernel(
    g_ref, m_ref, nm_ref, up_ref,
    graw, s_ref, ga, gb, g, a2, ah, al, ph, plo, bh, bl, work, theirs, leave,
    acc, rl, rs, mbuf, dx, dh, dl, packed, ra1, rb1, ra2, rb2, share, rz, piece, gz,
    msem, gsem, ls, lr, ss, sr, als, alr, ass, asr, cs, cr,
    a1s, a1r, b1s, b1r, a2s, a2r, b2s, b2r, z1s, z1r, z2s, z2r,
    ga1s, ga1r, gb1s, gb1r, ga2s, ga2r, gb2s, gb2r, gcs, gcr, dsem, usem,
):
    z = lax.axis_index("dp")
    f = lax.axis_index("fsdp")
    c = f % 2
    y = (f // 2) % 4
    x = f // 8
    layer = z // 4
    q = z % 4
    other = device(x, y, z, 1 - c)
    way = 1 - 2 * c
    up = device(x, y, (z + way + NZ) % NZ, c)
    down = device(x, y, (z - way + NZ) % NZ, c)

    def chunk(offset):
        return (z + way * offset + 2 * NZ) % NZ

    load = pltpu.make_async_copy(g_ref, graw, gsem)
    load.start()
    fetch = pltpu.make_async_copy(m_ref, mbuf, msem)
    fetch.start()

    barrier = pltpu.get_barrier_semaphore()
    greeted = [other]
    greeted += [device(x, y, (z + o) % NZ, c) for o in range(1, NZ)]
    greeted += [device((x + o) % 4, y, z, c) for o in range(1, 4)]
    greeted += [device(x, (y + o) % 4, z, c) for o in range(1, 4)]
    for target in greeted:
        pl.semaphore_signal(barrier, inc=1, device_id=target, device_id_type=MESH)
    load.wait()
    for i in range(4):
        rows = graw[i * 2 * CH : (i + 1) * 2 * CH, :].astype(F32)
        acc[2 * i] = rows[:CH]
        acc[2 * i + 1] = rows[CH:]
    pl.semaphore_wait(barrier, len(greeted))

    def cols(k):
        return pl.ds(k * W, W)

    started = []

    def go(copy):
        copy.start()
        started.append(copy)
        return copy

    def long_hop(step, k):
        return remote(acc.at[chunk(4 - step), :, cols(k)], rl.at[step, :, cols(k)], ls.at[step, k], lr.at[step, k], up)

    def short_hop(step, k):
        return remote(acc.at[chunk(step - 3), :, cols(k)], rs.at[step, :, cols(k)], ss.at[step, k], sr.at[step, k], down)

    hops = {}
    for k in range(SUB):
        hops["l", 0, k] = go(long_hop(0, k))
        hops["s", 0, k] = go(short_hop(0, k))
    for step in range(1, 4):
        for k in range(SUB):
            hops["l", step - 1, k].wait_recv()
            at = chunk(4 - step)
            acc[at, :, cols(k)] = acc[at, :, cols(k)] + rl[step - 1, :, cols(k)]
            hops["l", step, k] = go(long_hop(step, k))
            if step < 3:
                hops["s", step - 1, k].wait_recv()
                at = chunk(step - 3)
                acc[at, :, cols(k)] = acc[at, :, cols(k)] + rs[step - 1, :, cols(k)]
                hops["s", step, k] = go(short_hop(step, k))

    def gather_up(step, k):
        at = chunk(-step)
        return remote(s_ref.at[at, :, cols(k)], s_ref.at[at, :, cols(k)], als.at[step, k], alr.at[step, k], up)

    def gather_down(step, k):
        at = chunk(step)
        return remote(s_ref.at[at, :, cols(k)], s_ref.at[at, :, cols(k)], ass.at[step, k], asr.at[step, k], down)

    fetch.wait()
    mine = []
    for k in range(SUB):
        hops["s", 2, k].wait_recv()
        hops["l", 3, k].wait_recv()
        total = acc[z, :, cols(k)] + rs[2, :, cols(k)] + rl[3, :, cols(k)]
        s_ref[z, :, cols(k)] = total
        d = total + MOMENTUM_FACTOR * (MOMENTUM_FACTOR * mbuf[z, :, cols(k)] + total)
        dx[0:CH, cols(k)] = d
        mine.append(
            go(remote(dx.at[pl.ds(0, CH), cols(k)], dx.at[pl.ds(CH, CH), cols(k)], cs.at[k], cr.at[k], other))
        )
        hops["u", 0, k] = go(gather_up(0, k))
        hops["d", 0, k] = go(gather_down(0, k))

    for k in range(SUB):
        mine[k].wait_recv()
        d = dx[:, cols(k)]
        hi = d.astype(BF16)
        lo = (d - hi.astype(F32)).astype(BF16)
        dh[:, cols(k)] = hi
        dl[:, cols(k)] = lo
        if k == 0:
            dh[:, R : R + W] = hi
            dl[:, R : R + W] = lo

    def gram(first, second, width):
        li = pl.ds(pl.multiple_of(first * 128, 128), 128)
        ri = pl.ds(pl.multiple_of(second * 128, 128), width)

        def dot(left, right):
            return lax.dot_general(left, right, (((0,), (0,)), ((), ())), preferred_element_type=F32)

        lh, ll, rh, rlo = dh[:, li], dl[:, li], dh[:, ri], dl[:, ri]
        return dot(lh, rh) + (dot(lh, rlo) + dot(ll, rh))

    for a in range(3):
        block = gram(3 * c + a, 3 * c + a, 384)
        for k in range(3):
            packed[(3 * a + k) * 128 : (3 * a + k + 1) * 128, :] = block[:, k * 128 : (k + 1) * 128]
    for b in range(2):
        packed[(9 + b) * 128 : (10 + b) * 128, :] = gram(2 * c + b, 2 * c + b + 3, 128)

    pa = (x * (1 - c) + y * c, y * (1 - c) + x * c)
    pb = (pa[1], pa[0])

    def on_a(first, second):
        return device(first * (1 - c) + second * c, second * (1 - c) + first * c, z, c)

    def on_b(first, second):
        return on_a(second, first)

    paths = (
        (0, BA, pa, on_a, ra1, ra2, a1s, a1r, a2s, a2r, ga, ga1s, ga1r, ga2s, ga2r),
        (SPLIT, BB, pb, on_b, rb1, rb2, b1s, b1r, b2s, b2r, gb, gb1s, gb1r, gb2s, gb2r),
    )
    order = (2, 1, 3)

    first_hops = []
    for base, rows, (p1, p2), on, r1, r2, s1, t1, s2, t2, *_ in paths:
        size = 4 * rows
        for o in order:
            to = (p1 + o) % 4
            src = packed.at[pl.ds(pl.multiple_of(base + to * size, 8), size)]
            first_hops.append(go(remote(src, r1.at[o - 1], s1.at[o - 1], t1.at[o - 1], on(to, p2))))

    for k in range(SUB):
        hops["u", 0, k].wait_recv()
        hops["u", 1, k] = go(gather_up(1, k))
        hops["d", 0, k].wait_recv()
        hops["d", 1, k] = go(gather_down(1, k))

    second_hops = []
    for n, (base, rows, (p1, p2), on, r1, r2, s1, t1, s2, t2, *_) in enumerate(paths):
        size = 4 * rows
        for hop in first_hops[3 * n : 3 * n + 3]:
            hop.wait_recv()
        own = pl.ds(pl.multiple_of(base + p1 * size, 8), size)
        r1[3] = (packed[own, :] + r1[0]) + (r1[1] + r1[2])
        for o in order:
            to = (p2 + o) % 4
            src = r1.at[3, pl.ds(pl.multiple_of(to * rows, 8), rows)]
            second_hops.append(go(remote(src, r2.at[o - 1], s2.at[o - 1], t2.at[o - 1], on(p1, to))))
    for n, (base, rows, (p1, p2), on, r1, r2, *_) in enumerate(paths):
        for hop in second_hops[3 * n : 3 * n + 3]:
            hop.wait_recv()
        own = pl.ds(pl.multiple_of(p2 * rows, 8), rows)
        start = 0 if n == 0 else BA
        share[start : start + rows, :] = (r1[3, own, :] + r2[0]) + (r2[1] + r2[2])
    share[BA + BB : 96, :] = jnp.zeros((96 - BA - BB, 128), F32)

    quarter = []
    for o in (2, 1, 3):
        to = (q + o) % 4
        src = share.at[pl.ds(pl.multiple_of(to * 24, 8), 24)]
        quarter.append(go(remote(src, rz.at[o - 1], z1s.at[o - 1], z1r.at[o - 1], device(x, y, layer * 4 + to, c))))
    for hop in quarter:
        hop.wait_recv()
    at = pl.ds(pl.multiple_of(q * 24, 8), 24)
    total = (share[at, :] + rz[0]) + (rz[1] + rz[2])
    piece[...] = total
    gz[layer, at, :] = total
    spread = []
    for o in (4, 3, 5, 2, 6, 1, 7):
        spread.append(
            go(remote(piece, gz.at[layer, at], z2s.at[o - 1], z2r.at[o - 1], device(x, y, (z + o) % NZ, c)))
        )
    for hop in spread:
        hop.wait_recv()

    near, far = [], []
    for n, (base, rows, (p1, p2), on, r1, r2, s1, t1, s2, t2, out, u1, v1, u2, v2) in enumerate(paths):
        start = 0 if n == 0 else BA
        out[c, p1, p2] = gz[:, start : start + rows, :]
        block = out.at[c, p1, p2]
        for o in order:
            near.append(go(remote(block, block, u1.at[o - 1], v1.at[o - 1], on(p1, (p2 + o) % 4))))
        for o in order:
            far.append(go(remote(block, block, u2.at[o - 1, 0], v2.at[o - 1, 0], on((p1 + o) % 4, p2))))

    for k in range(SUB):
        hops["u", 1, k].wait_recv()
        hops["u", 2, k] = go(gather_up(2, k))
        hops["d", 1, k].wait_recv()
        hops["d", 2, k] = go(gather_down(2, k))

    for i, o in enumerate(order):
        for n, (base, rows, (p1, p2), on, r1, r2, s1, t1, s2, t2, out, u1, v1, u2, v2) in enumerate(paths):
            near[3 * n + i].wait_recv()
            block = out.at[c, p1, (p2 + 4 - o) % 4]
            for e in order:
                far.append(go(remote(block, block, u2.at[e - 1, o], v2.at[e - 1, o], on((p1 + e) % 4, p2))))

    for k in range(SUB):
        hops["u", 2, k].wait_recv()
        hops["u", 3, k] = go(gather_up(3, k))

    crossing = []

    def cross(n, first, o):
        out = (ga, gb)[n]
        block = out.at[c, first, :, 1 - c]
        crossing.append(go(remote(block, block, gcs.at[n, o], gcr.at[n, o], other)))

    for n in range(2):
        cross(n, paths[n][2][0], 0)
    for i, o in enumerate(order):
        for n in range(2):
            far[3 * n + i].wait_recv()
            for j in range(3):
                far[6 + 6 * j + 3 * n + i].wait_recv()
            cross(n, (paths[n][2][0] + 4 - o) % 4, o)
    for hop in crossing:
        hop.wait_recv()

    trace = jnp.zeros((), F32)
    eye = lax.broadcasted_iota(jnp.int32, (128, 128), 0) == lax.broadcasted_iota(jnp.int32, (128, 128), 1)
    for h in range(2):
        rows_a = ga[h, :, :, c].reshape(16 * BA, 128)
        rows_b = gb[h, :, :, c].reshape(16 * BB, 128)
        for b in range(BLOCKS):
            if b < 9:
                i = 3 * h + b // 3
                j = (i + b % 3) % 6
            else:
                i = 2 * h + b - 9
                j = (i + 3) % 6
            if i == 3 and j == 0:
                continue
            block = rows_a[b * 128 : (b + 1) * 128] if b < 6 else rows_b[(b - 6) * 128 : (b - 5) * 128]
            g[i * 128 : (i + 1) * 128, j * 128 : (j + 1) * 128] = block
            if i == j:
                trace = trace + jnp.sum(jnp.where(eye, block, 0.0))
            else:
                g[j * 128 : (j + 1) * 128, i * 128 : (i + 1) * 128] = block.T
    inverse = 1.0 / (jnp.sqrt(jnp.broadcast_to(trace, (8, 128))) + NORM_EPSILON)
    scale = inverse[0:1, 0:1]
    a = g[...] * (scale * scale)
    g[...] = a
    ah[...], al[...] = split(a)
    symmetric_product(a2, ah, al, ah, al)

    for k in range(SUB):
        hops["d", 2, k].wait_recv()
        hops["u", 3, k].wait_recv()
    for i in range(NZ):
        nm_ref[i] = MOMENTUM_FACTOR * mbuf[i] + s_ref[i]
    for i in range(4):
        at = 4 * (1 - c) + i
        leave[i * CH : (i + 1) * CH, :] = s_ref[at] + MOMENTUM_FACTOR * nm_ref[at]
    handed = go(remote(leave, work.at[pl.ds(224, 224)], dsem.at[0], dsem.at[1], other))
    for i in range(4):
        at = 4 * c + i
        work[i * CH : (i + 1) * CH, :] = s_ref[at] + MOMENTUM_FACTOR * nm_ref[at]

    diagonal = lax.broadcasted_iota(jnp.int32, (R, R), 0) == lax.broadcasted_iota(jnp.int32, (R, R), 1)
    p = jnp.where(diagonal, QUINTIC_LINEAR, 0.0) + QUINTIC_CUBIC * g[...] + QUINTIC_FIFTH * a2[...]
    ph[...], plo[...] = split(p)
    symmetric_product(a2, ph, plo, ah, al)
    bh[...], bl[...] = split(a2[...])
    symmetric_product(g, ph, plo, bh, bl)
    ah[...], al[...] = split(g[...])

    handed.wait_recv()
    x1 = dot3(split(work[...]), (ph[...], plo[...])) * scale
    second = (ah[...], al[...])
    y1 = dot3(split(x1), second)
    partial = QUINTIC_LINEAR * x1 + QUINTIC_CUBIC * y1
    factor = UPDATE_FACTOR * math.sqrt(max(D, R))
    theirs[...] = factor * (partial[224:] + QUINTIC_FIFTH * dot3(split(y1[224:]), second))
    back = go(remote(theirs, up_ref.at[c], usem.at[0], usem.at[1], other))
    up_ref[c] = factor * (partial[:224] + QUINTIC_FIFTH * dot3(split(y1[:224]), second))
    back.wait_recv()
    for copy in started:
        copy.wait_send()


def split(value):
    hi = value.astype(BF16)
    return hi, (value - hi.astype(F32)).astype(BF16)


def dot3(left, right):
    (lh, ll), (rh, rl) = left, right

    def dot(a, b):
        return jnp.dot(a, b, preferred_element_type=F32)

    return dot(lh, rh) + (dot(lh, rl) + dot(ll, rh))


def symmetric_product(out, lh, ll, rh, rl):
    for j in range(3):
        rows = slice(0, (j + 1) * 256)
        at = slice(j * 256, (j + 1) * 256)
        block = dot3((lh[rows, :], ll[rows, :]), (rh[:, at], rl[:, at]))
        out[rows, at] = block
        for i in range(j):
            out[at, i * 256 : (i + 1) * 256] = block[i * 256 : (i + 1) * 256].T


def update_kernel(nm_ref, up_ref, w_ref, nm_out, up_out, nw_out, nw, sems):
    copies = [pltpu.make_async_copy(nm_ref, nm_out, sems.at[0]), pltpu.make_async_copy(up_ref, up_out, sems.at[1])]
    for copy in copies:
        copy.start()
    for i in range(4):
        rows = pl.ds(i * 112, 112)
        weights = w_ref[rows, :]
        nw[rows, :] = weights - LEARNING_RATE * (up_ref[rows, :] + WEIGHT_DECAY * weights)
        copies.append(pltpu.make_async_copy(nw.at[rows], nw_out.at[rows], sems.at[2 + i]))
        copies[-1].start()
    for copy in copies:
        copy.wait()


def shards(replica_grads, momentum, weights):
    grads = replica_grads.reshape(NZ * CH, R)
    momentum = momentum.reshape(NZ, CH, R)
    weights = weights.reshape(NZ * CH, R)
    vmem = pl.BlockSpec(memory_space=pltpu.VMEM)
    hbm = pl.BlockSpec(memory_space=pltpu.HBM)
    sem = pltpu.SemaphoreType.DMA
    square = pltpu.VMEM((R, R), F32)
    half = pltpu.VMEM((R, R), BF16)
    new_momentum, update = pl.pallas_call(
        gram_kernel,
        out_shape=(
            jax.ShapeDtypeStruct((NZ, CH, R), F32),
            jax.ShapeDtypeStruct((2, 224, R), F32),
        ),
        in_specs=[hbm, hbm],
        out_specs=(vmem, vmem),
        scratch_shapes=[
            pltpu.VMEM((NZ * CH, R), BF16),
            pltpu.VMEM((NZ, CH, R), F32),
            pltpu.VMEM((2, 4, 4, 2, BA, 128), F32),
            pltpu.VMEM((2, 4, 4, 2, BB, 128), F32),
            square, square, half, half, half, half, half, half,
            pltpu.VMEM((NZ * CH, R), F32),
            pltpu.VMEM((224, R), F32),
            pltpu.VMEM((224, R), F32),
            pltpu.VMEM((NZ, CH, R), F32),
            pltpu.VMEM((4, CH, R), F32),
            pltpu.VMEM((3, CH, R), F32),
            pltpu.VMEM((NZ, CH, R), F32),
            pltpu.VMEM((2 * CH, R), F32),
            pltpu.VMEM((2 * CH, R + W), BF16),
            pltpu.VMEM((2 * CH, R + W), BF16),
            pltpu.VMEM((BLOCKS * 128, 128), F32),
            pltpu.VMEM((4, 4 * BA, 128), F32),
            pltpu.VMEM((4, 4 * BB, 128), F32),
            pltpu.VMEM((3, BA, 128), F32),
            pltpu.VMEM((3, BB, 128), F32),
            pltpu.VMEM((96, 128), F32),
            pltpu.VMEM((3, 24, 128), F32),
            pltpu.VMEM((24, 128), F32),
            pltpu.VMEM((2, 96, 128), F32),
            sem,
            sem,
        ]
        + [sem((4, SUB)), sem((4, SUB)), sem((3, SUB)), sem((3, SUB))] * 2
        + [sem((SUB,))] * 2
        + [sem((3,))] * 10
        + [sem((7,))] * 2
        + [sem((3,))] * 4
        + [sem((3, 4))] * 4
        + [sem((2, 4))] * 2
        + [sem((2,))] * 2,
        compiler_params=pltpu.CompilerParams(collective_id=0, has_side_effects=True, vmem_limit_bytes=34 << 20),
        name="gram",
    )(grads, momentum)
    like = jax.ShapeDtypeStruct((NZ * CH, R), F32)
    outs = pl.pallas_call(
        update_kernel,
        out_shape=(like, like, like),
        in_specs=[vmem] * 3,
        out_specs=(hbm, hbm, hbm),
        scratch_shapes=[pltpu.VMEM((NZ * CH, R), F32), sem((6,))],
        compiler_params=pltpu.CompilerParams(vmem_limit_bytes=4 << 20),
        name="update",
    )(new_momentum.reshape(NZ * CH, R), update.reshape(NZ * CH, R), weights)
    return tuple(o.reshape(2, 224, R) for o in outs)


def solution(mesh):
    return jax.shard_map(
        shards,
        mesh=mesh,
        in_specs=(P("dp", None, "fsdp", None), P(None, "fsdp", None), P(None, "fsdp", None)),
        out_specs=(P(None, "fsdp", None), P(None, "fsdp", None), P(None, "fsdp", None)),
        check_vma=False,
    )
```

```python
import functools
import math

import jax
import jax.numpy as jnp
from jax import lax
from jax.experimental import pallas as pl
from jax.experimental.pallas import tpu as pltpu
from jax.sharding import PartitionSpec as P

D = 7168
R = 768

QUINTIC_LINEAR = 3.4445
QUINTIC_CUBIC = -4.775
QUINTIC_FIFTH = 2.0315
MOMENTUM_FACTOR = 0.95
LEARNING_RATE = 0.02
WEIGHT_DECAY = 0.1
NORM_EPSILON = 1e-07
UPDATE_FACTOR = 0.2

MESH = pl.DeviceIdType.MESH
F32 = jnp.float32
BF16 = jnp.bfloat16
NZ = 8
CH = 56
SUB = 3
W = R // SUB
BA, BB = 48, 40
BLOCKS = 11
SPLIT = 16 * BA


def device(x, y, z, c):
    return (z, (x * 4 + y) * 2 + c)


def remote(src, dst, send, recv, target):
    return pltpu.make_async_remote_copy(
        src_ref=src, dst_ref=dst, send_sem=send, recv_sem=recv, device_id=target, device_id_type=MESH
    )


def gram_kernel(
    g_ref, m_ref, nm_ref, up_ref,
    graw, s_ref, ga, gb, g, ah, al, ph, plo, bh, bl, wh, wl, xh, xl, work, theirs, leave,
    acc, rl, rs, mbuf, dx, dh, dl, packed, ra1, rb1, ra2, rb2, share, rz, piece, gz,
    msem, gsem, ls, lr, ss, sr, als, alr, ass, asr, cs, cr,
    a1s, a1r, b1s, b1r, a2s, a2r, b2s, b2r, z1s, z1r, z2s, z2r,
    ga1s, ga1r, gb1s, gb1r, ga2s, ga2r, gb2s, gb2r, gcs, gcr, dsem, usem, ready,
):
    z = lax.axis_index("dp")
    f = lax.axis_index("fsdp")
    c = f % 2
    y = (f // 2) % 4
    x = f // 8
    layer = z // 4
    q = z % 4
    other = device(x, y, z, 1 - c)
    way = 1 - 2 * c
    up = device(x, y, (z + way + NZ) % NZ, c)
    down = device(x, y, (z - way + NZ) % NZ, c)

    def chunk(offset):
        return (z + way * offset + 2 * NZ) % NZ

    load = pltpu.make_async_copy(g_ref, graw, gsem)
    load.start()
    fetch = pltpu.make_async_copy(m_ref, mbuf, msem)
    fetch.start()

    barrier = pltpu.get_barrier_semaphore()
    greeted = [other]
    greeted += [device(x, y, (z + o) % NZ, c) for o in (1, NZ - 1)]
    beside = [device((x + o) % 4, y, z, c) for o in (1, 3)] + [device(x, (y + o) % 4, z, c) for o in (1, 3)]
    greeted += beside
    for target in greeted:
        pl.semaphore_signal(barrier, inc=1, device_id=target, device_id_type=MESH)
    load.wait()
    for i in range(4):
        rows = graw[i * 2 * CH : (i + 1) * 2 * CH, :].astype(F32)
        acc[2 * i] = rows[:CH]
        acc[2 * i + 1] = rows[CH:]
    pl.semaphore_wait(barrier, len(greeted))
    for target in beside:
        pl.semaphore_signal(ready, inc=1, device_id=target, device_id_type=MESH)

    def cols(k):
        return pl.ds(k * W, W)

    started = []

    def go(copy):
        copy.start()
        started.append(copy)
        return copy

    def long_hop(step, k):
        return remote(acc.at[chunk(4 - step), :, cols(k)], rl.at[step, :, cols(k)], ls.at[step, k], lr.at[step, k], up)

    def short_hop(step, k):
        return remote(acc.at[chunk(step - 3), :, cols(k)], rs.at[step, :, cols(k)], ss.at[step, k], sr.at[step, k], down)

    hops = {}
    for k in range(SUB):
        hops["l", 0, k] = go(long_hop(0, k))
        hops["s", 0, k] = go(short_hop(0, k))
    for step in range(1, 4):
        for k in range(SUB):
            hops["l", step - 1, k].wait_recv()
            at = chunk(4 - step)
            acc[at, :, cols(k)] = acc[at, :, cols(k)] + rl[step - 1, :, cols(k)]
            hops["l", step, k] = go(long_hop(step, k))
            if step < 3:
                hops["s", step - 1, k].wait_recv()
                at = chunk(step - 3)
                acc[at, :, cols(k)] = acc[at, :, cols(k)] + rs[step - 1, :, cols(k)]
                hops["s", step, k] = go(short_hop(step, k))

    def gather_up(step, k):
        at = chunk(-step)
        return remote(s_ref.at[at, :, cols(k)], s_ref.at[at, :, cols(k)], als.at[step, k], alr.at[step, k], up)

    def gather_down(step, k):
        at = chunk(step)
        return remote(s_ref.at[at, :, cols(k)], s_ref.at[at, :, cols(k)], ass.at[step, k], asr.at[step, k], down)

    fetch.wait()
    mine = []
    for k in range(SUB):
        hops["s", 2, k].wait_recv()
        hops["l", 3, k].wait_recv()
        total = acc[z, :, cols(k)] + rs[2, :, cols(k)] + rl[3, :, cols(k)]
        s_ref[z, :, cols(k)] = total
        d = total + MOMENTUM_FACTOR * (MOMENTUM_FACTOR * mbuf[z, :, cols(k)] + total)
        dx[0:CH, cols(k)] = d
        mine.append(
            go(remote(dx.at[pl.ds(0, CH), cols(k)], dx.at[pl.ds(CH, CH), cols(k)], cs.at[k], cr.at[k], other))
        )
        hops["u", 0, k] = go(gather_up(0, k))
        hops["d", 0, k] = go(gather_down(0, k))

    for k in range(SUB):
        mine[k].wait_recv()
        d = dx[:, cols(k)]
        hi = d.astype(BF16)
        lo = (d - hi.astype(F32)).astype(BF16)
        dh[:, cols(k)] = hi
        dl[:, cols(k)] = lo
        if k == 0:
            dh[:, R : R + W] = hi
            dl[:, R : R + W] = lo

    def gram(first, second, width):
        li = pl.ds(pl.multiple_of(first * 128, 128), 128)
        ri = pl.ds(pl.multiple_of(second * 128, 128), width)

        def dot(left, right):
            return lax.dot_general(left, right, (((0,), (0,)), ((), ())), preferred_element_type=F32)

        lh, ll, rh, rlo = dh[:, li], dl[:, li], dh[:, ri], dl[:, ri]
        return dot(lh, rh) + (dot(lh, rlo) + dot(ll, rh))

    def row_blocks(a):
        block = gram(3 * c + a, 3 * c + a, 384)
        for k in range(3):
            packed[(3 * a + k) * 128 : (3 * a + k + 1) * 128, :] = block[:, k * 128 : (k + 1) * 128]

    row_blocks(0)
    row_blocks(1)

    pa = (x * (1 - c) + y * c, y * (1 - c) + x * c)
    pb = (pa[1], pa[0])

    def on_a(first, second):
        return device(first * (1 - c) + second * c, second * (1 - c) + first * c, z, c)

    def on_b(first, second):
        return on_a(second, first)

    paths = (
        (0, BA, pa, on_a, ra1, ra2, a1s, a1r, a2s, a2r, ga, ga1s, ga1r, ga2s, ga2r),
        (SPLIT, BB, pb, on_b, rb1, rb2, b1s, b1r, b2s, b2r, gb, gb1s, gb1r, gb2s, gb2r),
    )
    order = (2, 1, 3)

    first_hops = []

    def start_first(base, rows, at, on, r1, r2, s1, t1, *_):
        size = 4 * rows
        for o in order:
            to = (at[0] + o) % 4
            src = packed.at[pl.ds(pl.multiple_of(base + to * size, 8), size)]
            first_hops.append(go(remote(src, r1.at[o - 1], s1.at[o - 1], t1.at[o - 1], on(to, at[1]))))

    pl.semaphore_wait(ready, len(beside))
    start_first(*paths[0])
    row_blocks(2)
    for b in range(2):
        packed[(9 + b) * 128 : (10 + b) * 128, :] = gram(2 * c + b, 2 * c + b + 3, 128)
    start_first(*paths[1])

    for k in range(SUB):
        hops["u", 0, k].wait_recv()
        hops["u", 1, k] = go(gather_up(1, k))
        hops["d", 0, k].wait_recv()
        hops["d", 1, k] = go(gather_down(1, k))

    second_hops = []
    for n, (base, rows, (p1, p2), on, r1, r2, s1, t1, s2, t2, *_) in enumerate(paths):
        size = 4 * rows
        for hop in first_hops[3 * n : 3 * n + 3]:
            hop.wait_recv()
        own = pl.ds(pl.multiple_of(base + p1 * size, 8), size)
        r1[3] = (packed[own, :] + r1[0]) + (r1[1] + r1[2])
        for o in order:
            to = (p2 + o) % 4
            src = r1.at[3, pl.ds(pl.multiple_of(to * rows, 8), rows)]
            second_hops.append(go(remote(src, r2.at[o - 1], s2.at[o - 1], t2.at[o - 1], on(p1, to))))
    for n, (base, rows, (p1, p2), on, r1, r2, *_) in enumerate(paths):
        for hop in second_hops[3 * n : 3 * n + 3]:
            hop.wait_recv()
        own = pl.ds(pl.multiple_of(p2 * rows, 8), rows)
        start = 0 if n == 0 else BA
        share[start : start + rows, :] = (r1[3, own, :] + r2[0]) + (r2[1] + r2[2])
    share[BA + BB : 96, :] = jnp.zeros((96 - BA - BB, 128), F32)

    quarter = []
    for o in (2, 1, 3):
        to = (q + o) % 4
        src = share.at[pl.ds(pl.multiple_of(to * 24, 8), 24)]
        quarter.append(go(remote(src, rz.at[o - 1], z1s.at[o - 1], z1r.at[o - 1], device(x, y, layer * 4 + to, c))))
    for hop in quarter:
        hop.wait_recv()
    at = pl.ds(pl.multiple_of(q * 24, 8), 24)
    total = (share[at, :] + rz[0]) + (rz[1] + rz[2])
    piece[...] = total
    gz[layer, at, :] = total
    for o in (4, 3, 5, 2, 6, 1, 7):
        go(remote(piece, gz.at[layer, at], z2s.at[o - 1], z2r.at[z], device(x, y, (z + o) % NZ, c)))

    near, far = [], []

    def start_gather(n, base, rows, at, on, r1, r2, s1, t1, s2, t2, out, u1, v1, u2, v2):
        for plane in (2 * n, 2 * n + 1, 2 * n + 4, 2 * n + 5):

            @pl.when(z != plane)
            def _():
                land = gz.at[plane // 4, pl.ds(plane % 4 * 24, 24)]
                remote(piece, land, z2s.at[0], z2r.at[plane], other).wait_recv()

        p1, p2 = at
        start = 0 if n == 0 else BA
        out[c, p1, p2] = gz[:, start : start + rows, :]
        block = out.at[c, p1, p2]
        for o in order:
            near.append(go(remote(block, block, u1.at[o - 1], v1.at[o - 1], on(p1, (p2 + o) % 4))))
        for o in order:
            far.append(go(remote(block, block, u2.at[o - 1, 0], v2.at[o - 1, 0], on((p1 + o) % 4, p2))))

    for n in range(2):
        start_gather(n, *paths[n])

    for k in range(SUB):
        hops["u", 1, k].wait_recv()
        hops["u", 2, k] = go(gather_up(2, k))
        hops["d", 1, k].wait_recv()
        hops["d", 2, k] = go(gather_down(2, k))

    for i, o in enumerate(order):
        for n, (base, rows, (p1, p2), on, r1, r2, s1, t1, s2, t2, out, u1, v1, u2, v2) in enumerate(paths):
            near[3 * n + i].wait_recv()
            block = out.at[c, p1, (p2 + 4 - o) % 4]
            for e in order:
                far.append(go(remote(block, block, u2.at[e - 1, o], v2.at[e - 1, o], on((p1 + e) % 4, p2))))

    for k in range(SUB):
        hops["u", 2, k].wait_recv()
        hops["u", 3, k] = go(gather_up(3, k))

    crossing = []

    def cross(n, first, o):
        out = (ga, gb)[n]
        block = out.at[c, first, :, 1 - c]
        crossing.append(go(remote(block, block, gcs.at[n, o], gcr.at[n, o], other)))

    for n in range(2):
        cross(n, paths[n][2][0], 0)
    for i, o in enumerate(order):
        for n in range(2):
            far[3 * n + i].wait_recv()
            for j in range(3):
                far[6 + 6 * j + 3 * n + i].wait_recv()
            cross(n, (paths[n][2][0] + 4 - o) % 4, o)
    for hop in crossing:
        hop.wait_recv()

    trace = jnp.zeros((), F32)
    eye = lax.broadcasted_iota(jnp.int32, (128, 128), 0) == lax.broadcasted_iota(jnp.int32, (128, 128), 1)
    for h in range(2):
        rows_a = ga[h, :, :, c].reshape(16 * BA, 128)
        rows_b = gb[h, :, :, c].reshape(16 * BB, 128)
        for b in range(BLOCKS):
            if b < 9:
                i = 3 * h + b // 3
                j = (i + b % 3) % 6
            else:
                i = 2 * h + b - 9
                j = (i + 3) % 6
            if i == 3 and j == 0:
                continue
            block = rows_a[b * 128 : (b + 1) * 128] if b < 6 else rows_b[(b - 6) * 128 : (b - 5) * 128]
            g[i * 128 : (i + 1) * 128, j * 128 : (j + 1) * 128] = block
            if i == j:
                trace = trace + jnp.sum(jnp.where(eye, block, 0.0))
            else:
                g[j * 128 : (j + 1) * 128, i * 128 : (i + 1) * 128] = block.T
    inverse = 1.0 / (jnp.sqrt(jnp.broadcast_to(trace, (8, 128))) + NORM_EPSILON)
    scale = inverse[0:1, 0:1]
    square = scale * scale
    for j in range(3):
        put(ah, al, slice(0, R), COLS[j], g[:, COLS[j]] * square)
    corner = lax.broadcasted_iota(jnp.int32, (256, 256), 0) == lax.broadcasted_iota(jnp.int32, (256, 256), 1)
    linear = jnp.where(corner, QUINTIC_LINEAR, 0.0)

    def polynomial(value, i, j):
        value = (QUINTIC_CUBIC * square) * g[COLS[i], COLS[j]] + QUINTIC_FIFTH * value
        return linear + value if i == j else value

    symmetric_product((ah, al), (ah, al), (ph, plo), polynomial)

    for k in range(SUB):
        hops["d", 2, k].wait_recv()
        hops["u", 3, k].wait_recv()
    for i in range(NZ):
        nm_ref[i] = MOMENTUM_FACTOR * mbuf[i] + s_ref[i]
    for i in range(4):
        at = 4 * (1 - c) + i
        leave[i * CH : (i + 1) * CH, :] = s_ref[at] + MOMENTUM_FACTOR * nm_ref[at]
    handed = go(remote(leave, work.at[pl.ds(224, 224)], dsem.at[0], dsem.at[1], other))
    for i in range(4):
        at = 4 * c + i
        work[i * CH : (i + 1) * CH, :] = s_ref[at] + MOMENTUM_FACTOR * nm_ref[at]

    symmetric_product((ph, plo), (ah, al), (bh, bl))
    symmetric_product((ph, plo), (bh, bl), (ah, al))

    handed.wait_recv()
    factor = UPDATE_FACTOR * math.sqrt(max(D, R))
    halves = (slice(224, 448), slice(0, 224))
    every = slice(0, R)
    for rows in halves:
        put(wh, wl, rows, every, work[rows, :])
    for rows in halves:
        x1 = dot3((wh[rows, :], wl[rows, :]), (ph[...], plo[...])) * scale
        work[rows, :] = QUINTIC_LINEAR * x1
        put(xh, xl, rows, every, x1)
    for rows in halves:
        y1 = dot3((xh[rows, :], xl[rows, :]), (ah[...], al[...]))
        work[rows, :] = work[rows, :] + QUINTIC_CUBIC * y1
        put(wh, wl, rows, every, y1)

    def finish(rows):
        return factor * (work[rows, :] + QUINTIC_FIFTH * dot3((wh[rows, :], wl[rows, :]), (ah[...], al[...])))

    theirs[...] = finish(halves[0])
    back = go(remote(theirs, up_ref.at[c], usem.at[0], usem.at[1], other))
    up_ref[c] = finish(halves[1])
    back.wait_recv()
    for copy in started:
        copy.wait_send()


def dot3(left, right):
    (lh, ll), (rh, rl) = left, right

    def dot(a, b):
        return jnp.dot(a, b, preferred_element_type=F32)

    return dot(lh, rh) + (dot(lh, rl) + dot(ll, rh))


def put(hi_ref, lo_ref, rows, cols, value):
    hi = value.astype(BF16)
    hi_ref[rows, cols] = hi
    lo_ref[rows, cols] = (value - hi.astype(F32)).astype(BF16)


COLS = [slice(j * 256, (j + 1) * 256) for j in range(3)]


def symmetric_product(left, right, out, then=None):
    (lh, ll), (rh, rl) = left, right
    for j in range(3):
        rows = slice(0, (j + 1) * 256)
        block = dot3((lh[rows, :], ll[rows, :]), (rh[:, COLS[j]], rl[:, COLS[j]]))
        for i in range(j + 1):
            value = block[COLS[i]]
            if then is not None:
                value = then(value, i, j)
            put(*out, COLS[i], COLS[j], value)
            if i < j:
                put(*out, COLS[j], COLS[i], value.T)


def update_kernel(nm_ref, up_ref, w_ref, nm_out, up_out, nw_out, nw, sems):
    copies = [pltpu.make_async_copy(nm_ref, nm_out, sems.at[0]), pltpu.make_async_copy(up_ref, up_out, sems.at[1])]
    for copy in copies:
        copy.start()
    for i in range(4):
        rows = pl.ds(i * 112, 112)
        weights = w_ref[rows, :]
        nw[rows, :] = weights - LEARNING_RATE * (up_ref[rows, :] + WEIGHT_DECAY * weights)
        copies.append(pltpu.make_async_copy(nw.at[rows], nw_out.at[rows], sems.at[2 + i]))
        copies[-1].start()
    for copy in copies:
        copy.wait()


def shards(replica_grads, momentum, weights):
    grads = pltpu.with_memory_space_constraint(replica_grads.reshape(NZ * CH, R), pltpu.HBM)
    momentum = pltpu.with_memory_space_constraint(momentum.reshape(NZ, CH, R), pltpu.HBM)
    weights = weights.reshape(NZ * CH, R)
    vmem = pl.BlockSpec(memory_space=pltpu.VMEM)
    hbm = pl.BlockSpec(memory_space=pltpu.HBM)
    sem = pltpu.SemaphoreType.DMA
    rows = pltpu.VMEM((NZ * CH, R), BF16)
    half = pltpu.VMEM((R, R), BF16)
    new_momentum, update = pl.pallas_call(
        gram_kernel,
        out_shape=(
            jax.ShapeDtypeStruct((NZ, CH, R), F32),
            jax.ShapeDtypeStruct((2, 224, R), F32),
        ),
        in_specs=[hbm, hbm],
        out_specs=(vmem, vmem),
        scratch_shapes=[
            pltpu.VMEM((NZ * CH, R), BF16),
            pltpu.VMEM((NZ, CH, R), F32),
            pltpu.VMEM((2, 4, 4, 2, BA, 128), F32),
            pltpu.VMEM((2, 4, 4, 2, BB, 128), F32),
            pltpu.VMEM((R, R), F32), half, half, half, half, half, half, rows, rows, rows, rows,
            pltpu.VMEM((NZ * CH, R), F32),
            pltpu.VMEM((224, R), F32),
            pltpu.VMEM((224, R), F32),
            pltpu.VMEM((NZ, CH, R), F32),
            pltpu.VMEM((4, CH, R), F32),
            pltpu.VMEM((3, CH, R), F32),
            pltpu.VMEM((NZ, CH, R), F32),
            pltpu.VMEM((2 * CH, R), F32),
            pltpu.VMEM((2 * CH, R + W), BF16),
            pltpu.VMEM((2 * CH, R + W), BF16),
            pltpu.VMEM((BLOCKS * 128, 128), F32),
            pltpu.VMEM((4, 4 * BA, 128), F32),
            pltpu.VMEM((4, 4 * BB, 128), F32),
            pltpu.VMEM((3, BA, 128), F32),
            pltpu.VMEM((3, BB, 128), F32),
            pltpu.VMEM((96, 128), F32),
            pltpu.VMEM((3, 24, 128), F32),
            pltpu.VMEM((24, 128), F32),
            pltpu.VMEM((2, 96, 128), F32),
            sem,
            sem,
        ]
        + [sem((4, SUB)), sem((4, SUB)), sem((3, SUB)), sem((3, SUB))] * 2
        + [sem((SUB,))] * 2
        + [sem((3,))] * 10
        + [sem((8,))] * 2
        + [sem((3,))] * 4
        + [sem((3, 4))] * 4
        + [sem((2, 4))] * 2
        + [sem((2,))] * 2
        + [pltpu.SemaphoreType.REGULAR],
        compiler_params=pltpu.CompilerParams(collective_id=0, has_side_effects=True, vmem_limit_bytes=34 << 20),
        name="gram",
    )(grads, momentum)
    like = jax.ShapeDtypeStruct((NZ * CH, R), F32)
    outs = pl.pallas_call(
        update_kernel,
        out_shape=(like, like, like),
        in_specs=[vmem] * 3,
        out_specs=(hbm, hbm, hbm),
        scratch_shapes=[pltpu.VMEM((NZ * CH, R), F32), sem((6,))],
        compiler_params=pltpu.CompilerParams(vmem_limit_bytes=4 << 20),
        name="update",
    )(new_momentum.reshape(NZ * CH, R), update.reshape(NZ * CH, R), weights)
    return tuple(o.reshape(2, 224, R) for o in outs)


def solution(mesh):
    return jax.shard_map(
        shards,
        mesh=mesh,
        in_specs=(P("dp", None, "fsdp", None), P(None, "fsdp", None), P(None, "fsdp", None)),
        out_specs=(P(None, "fsdp", None), P(None, "fsdp", None), P(None, "fsdp", None)),
        check_vma=False,
    )
```

```python
import functools
import math

import jax
import jax.numpy as jnp
from jax import lax
from jax.experimental import pallas as pl
from jax.experimental.pallas import tpu as pltpu
from jax.sharding import PartitionSpec as P

D = 7168
R = 768

QUINTIC_LINEAR = 3.4445
QUINTIC_CUBIC = -4.775
QUINTIC_FIFTH = 2.0315
MOMENTUM_FACTOR = 0.95
LEARNING_RATE = 0.02
WEIGHT_DECAY = 0.1
NORM_EPSILON = 1e-07
UPDATE_FACTOR = 0.2

MESH = pl.DeviceIdType.MESH
F32 = jnp.float32
BF16 = jnp.bfloat16
NZ = 8
CH = 56
SUB = 3
W = R // SUB
BA, BB = 48, 40
BLOCKS = 11
SPLIT = 16 * BA


def device(x, y, z, c):
    return (z, (x * 4 + y) * 2 + c)


def remote(src, dst, send, recv, target):
    return pltpu.make_async_remote_copy(
        src_ref=src, dst_ref=dst, send_sem=send, recv_sem=recv, device_id=target, device_id_type=MESH
    )


def gram_kernel(
    g_ref, m_ref, nm_ref, up_ref,
    graw, s_ref, ga, gb, g, ah, al, ph, plo, bh, bl, wh, wl, xh, xl, work, theirs, dall, dother,
    acc, rl, rs, mbuf, dx, dh, dl, packed, ra1, rb1, half, rz, piece, gz,
    msem, gsem, ls, lr, ss, sr, als, alr, ass, asr, cs, cr,
    a1s, a1r, b1s, b1r, ms, mr, z2s, z2r,
    ga1s, ga1r, gb1s, gb1r, ga2s, ga2r, gb2s, gb2r, gcs, gcr, dsem, usem, ready, summed,
):
    z = lax.axis_index("dp")
    f = lax.axis_index("fsdp")
    c = f % 2
    y = (f // 2) % 4
    x = f // 8
    layer = z // 4
    q = z % 4
    other = device(x, y, z, 1 - c)
    way = 1 - 2 * c
    up = device(x, y, (z + way + NZ) % NZ, c)
    down = device(x, y, (z - way + NZ) % NZ, c)

    def chunk(offset):
        return (z + way * offset + 2 * NZ) % NZ

    load = pltpu.make_async_copy(g_ref, graw, gsem)
    load.start()
    fetch = pltpu.make_async_copy(m_ref, mbuf, msem)
    fetch.start()

    barrier = pltpu.get_barrier_semaphore()
    greeted = [other]
    greeted += [device(x, y, (z + o) % NZ, c) for o in (1, NZ - 1)]
    beside = [device((x + o) % 4, y, z, c) for o in (1, 3)] + [device(x, (y + o) % 4, z, c) for o in (1, 3)]
    greeted += beside
    for target in greeted:
        pl.semaphore_signal(barrier, inc=1, device_id=target, device_id_type=MESH)
    load.wait()
    for i in range(4):
        rows = graw[i * 2 * CH : (i + 1) * 2 * CH, :].astype(F32)
        acc[2 * i] = rows[:CH]
        acc[2 * i + 1] = rows[CH:]
    pl.semaphore_wait(barrier, len(greeted))
    for target in beside:
        pl.semaphore_signal(ready, inc=1, device_id=target, device_id_type=MESH)

    def cols(k):
        return pl.ds(k * W, W)

    started = []
    local = []

    def go(copy):
        copy.start()
        started.append(copy)
        return copy

    def long_hop(step, k):
        return remote(acc.at[chunk(4 - step), :, cols(k)], rl.at[step, :, cols(k)], ls.at[step, k], lr.at[step, k], up)

    def short_hop(step, k):
        return remote(acc.at[chunk(step - 3), :, cols(k)], rs.at[step, :, cols(k)], ss.at[step, k], sr.at[step, k], down)

    hops = {}
    for k in range(SUB):
        hops["l", 0, k] = go(long_hop(0, k))
        hops["s", 0, k] = go(short_hop(0, k))
    for step in range(1, 4):
        for k in range(SUB):
            hops["l", step - 1, k].wait_recv()
            at = chunk(4 - step)
            acc[at, :, cols(k)] = acc[at, :, cols(k)] + rl[step - 1, :, cols(k)]
            hops["l", step, k] = go(long_hop(step, k))
            if step < 3:
                hops["s", step - 1, k].wait_recv()
                at = chunk(step - 3)
                acc[at, :, cols(k)] = acc[at, :, cols(k)] + rs[step - 1, :, cols(k)]
                hops["s", step, k] = go(short_hop(step, k))

    def gather_up(step, k):
        at = chunk(-step)
        return remote(s_ref.at[at, :, cols(k)], s_ref.at[at, :, cols(k)], als.at[step, k], alr.at[step, k], up)

    def gather_down(step, k):
        at = chunk(step)
        return remote(s_ref.at[at, :, cols(k)], s_ref.at[at, :, cols(k)], ass.at[step, k], asr.at[step, k], down)

    fetch.wait()
    mine = []
    for k in range(SUB):
        hops["s", 2, k].wait_recv()
        hops["l", 3, k].wait_recv()
        total = acc[z, :, cols(k)] + rs[2, :, cols(k)] + rl[3, :, cols(k)]
        s_ref[z, :, cols(k)] = total
        d = total + MOMENTUM_FACTOR * (MOMENTUM_FACTOR * mbuf[z, :, cols(k)] + total)
        dx[0:CH, cols(k)] = d
        mine.append(
            go(remote(dx.at[pl.ds(0, CH), cols(k)], dx.at[pl.ds(CH, CH), cols(k)], cs.at[k], cr.at[k], other))
        )
        hops["u", 0, k] = go(gather_up(0, k))
        hops["d", 0, k] = go(gather_down(0, k))

    pl.semaphore_wait(ready, len(beside))
    around = [device((x + o) % 4, y, z, c) for o in (1, 2, 3)] + [device(x, (y + o) % 4, z, c) for o in (1, 2, 3)]
    for target in around:
        pl.semaphore_signal(summed, inc=1, device_id=target, device_id_type=MESH)

    for k in range(SUB):
        mine[k].wait_recv()
        d = dx[:, cols(k)]
        hi = d.astype(BF16)
        lo = (d - hi.astype(F32)).astype(BF16)
        dh[:, cols(k)] = hi
        dl[:, cols(k)] = lo
        if k == 0:
            dh[:, R : R + W] = hi
            dl[:, R : R + W] = lo

    def gram(first, second, width):
        li = pl.ds(pl.multiple_of(first * 128, 128), 128)
        ri = pl.ds(pl.multiple_of(second * 128, 128), width)

        def dot(left, right):
            return lax.dot_general(left, right, (((0,), (0,)), ((), ())), preferred_element_type=F32)

        lh, ll, rh, rlo = dh[:, li], dl[:, li], dh[:, ri], dl[:, ri]
        return dot(lh, rh) + (dot(lh, rlo) + dot(ll, rh))

    def row_blocks(a):
        block = gram(3 * c + a, 3 * c + a, 384)
        for k in range(3):
            packed[(3 * a + k) * 128 : (3 * a + k + 1) * 128, :] = block[:, k * 128 : (k + 1) * 128]

    row_blocks(0)
    row_blocks(1)

    pa = (x * (1 - c) + y * c, y * (1 - c) + x * c)
    pb = (pa[1], pa[0])

    def on_a(first, second, plane):
        return device(first * (1 - c) + second * c, second * (1 - c) + first * c, plane, c)

    def on_b(first, second, plane):
        return on_a(second, first, plane)

    paths = (
        (0, BA, pa, on_a, ra1, a1s, a1r, ga, ga1s, ga1r, ga2s, ga2r),
        (SPLIT, BB, pb, on_b, rb1, b1s, b1r, gb, gb1s, gb1r, gb2s, gb2r),
    )
    order = (2, 1, 3)

    first_hops = []

    def start_first(base, rows, at, on, r1, s1, t1, *_):
        size = 4 * rows
        for o in order:
            to = (at[0] + o) % 4
            src = packed.at[pl.ds(pl.multiple_of(base + to * size, 8), size)]
            first_hops.append(go(remote(src, r1.at[o - 1], s1.at[o - 1], t1.at[o - 1], on(to, at[1], z))))

    start_first(*paths[0])
    row_blocks(2)
    for b in range(2):
        packed[(9 + b) * 128 : (10 + b) * 128, :] = gram(2 * c + b, 2 * c + b + 3, 128)
    start_first(*paths[1])

    def settle(offset):
        at = chunk(offset)
        nm_ref[at] = MOMENTUM_FACTOR * mbuf[at] + s_ref[at]
        dall[at] = s_ref[at] + MOMENTUM_FACTOR * nm_ref[at]

    settle(0)
    for k in range(SUB):
        hops["u", 0, k].wait_recv()
        hops["u", 1, k] = go(gather_up(1, k))
        hops["d", 0, k].wait_recv()
        hops["d", 1, k] = go(gather_down(1, k))

    pl.semaphore_wait(summed, len(around))
    for n, (base, rows, (p1, p2), on, r1, *_) in enumerate(paths):
        size = 4 * rows
        for hop in first_hops[3 * n : 3 * n + 3]:
            hop.wait_recv()
        own = pl.ds(pl.multiple_of(base + p1 * size, 8), size)
        total = (packed[own, :] + r1[0]) + (r1[1] + r1[2])
        for i in range(4):
            half[n, i, :rows] = total[i * rows : (i + 1) * rows]
            if rows < 48:
                half[n, i, rows:] = jnp.zeros((48 - rows, 128), F32)
        for o in (2, 1, 3, 0):
            to = (p2 + o) % 4
            for h in range(2):
                plane = 2 * n + h
                copy = remote(
                    half.at[n, to, pl.ds(24 * h, 24)], rz.at[4 * o + q], ms.at[n, o, h], mr.at[o, q],
                    on(p1, to, 4 * layer + plane),
                )
                if o > 0:
                    go(copy)
                else:
                    pl.when(q != plane)(copy.start)
                    local.append((q != plane, copy))
    settle(1)
    settle(-1)
    mine_n, mine_h = q // 2, q % 2
    mine_2 = pa[1] * (1 - mine_n) + pb[1] * mine_n
    rz[q] = half[mine_n, mine_2, pl.ds(pl.multiple_of(24 * mine_h, 8), 24)]
    for o in range(4):
        for plane in range(4):
            copy = remote(piece, rz.at[4 * o + plane], ms.at[0, 0, 0], mr.at[o, plane], other)
            if o > 0:
                copy.wait_recv()
            else:
                pl.when(q != plane)(copy.wait_recv)
    sums = [rz[i] for i in range(16)]
    while len(sums) > 1:
        sums = [sums[2 * i] + sums[2 * i + 1] for i in range(len(sums) // 2)]
    at = pl.ds(pl.multiple_of(q * 24, 8), 24)
    piece[...] = sums[0]
    gz[layer, at, :] = sums[0]
    for o in (4, 3, 5, 2, 6, 1, 7):
        go(remote(piece, gz.at[layer, at], z2s.at[o - 1], z2r.at[z], device(x, y, (z + o) % NZ, c)))

    layers = (layer, 1 - layer)
    near, far = {}, {}

    def start_far(t, n, j):
        base, rows, (p1, p2), on, r1, s1, t1, out, u1, v1, u2, v2 = paths[n]
        block = out.at[c, p1, (p2 + 4 - j) % 4, layers[t]]
        for o in order:
            far[t, n, o, j] = go(
                remote(block, block, u2.at[t, o - 1, j], v2.at[t, o - 1, j], on((p1 + o) % 4, p2, z))
            )

    for t in range(2):
        for n, (base, rows, (p1, p2), on, r1, s1, t1, out, u1, v1, u2, v2) in enumerate(paths):
            for h in range(2):
                plane = 4 * layers[t] + 2 * n + h
                land = gz.at[layers[t], pl.ds(48 * n + 24 * h, 24)]
                arrival = remote(piece, land, z2s.at[0], z2r.at[plane], other)
                if t == 0:
                    pl.when(z != plane)(arrival.wait_recv)
                else:
                    arrival.wait_recv()
            out[c, p1, p2, layers[t]] = gz[layers[t], 48 * n : 48 * n + rows, :]
            block = out.at[c, p1, p2, layers[t]]
            for o in order:
                near[t, n, o] = go(
                    remote(block, block, u1.at[t, o - 1], v1.at[t, o - 1], on(p1, (p2 + o) % 4, z))
                )
            start_far(t, n, 0)

    for k in range(SUB):
        hops["u", 1, k].wait_recv()
        hops["u", 2, k] = go(gather_up(2, k))
        hops["d", 1, k].wait_recv()
        hops["d", 2, k] = go(gather_down(2, k))
    settle(2)
    settle(-2)

    for t in range(2):
        for o in order:
            for n in range(2):
                near[t, n, o].wait_recv()
                start_far(t, n, o)

    for k in range(SUB):
        hops["u", 2, k].wait_recv()
        hops["u", 3, k] = go(gather_up(3, k))
    for k in range(SUB):
        hops["d", 2, k].wait_recv()
    settle(-3)
    settle(3)

    crossing = []

    def cross(n, first, o):
        out = (ga, gb)[n]
        block = out.at[c, first, :, 1 - c]
        crossing.append(go(remote(block, block, gcs.at[n, o], gcr.at[n, o], other)))

    for n in range(2):
        cross(n, paths[n][2][0], 0)
    for o in order:
        for n in range(2):
            for t in range(2):
                for j in range(4):
                    far[t, n, o, j].wait_recv()
            cross(n, (paths[n][2][0] + 4 - o) % 4, o)
    for k in range(SUB):
        hops["u", 3, k].wait_recv()
    settle(-4)
    handed = go(remote(dall.at[pl.ds(4 * (1 - c), 4)], dother, dsem.at[0], dsem.at[1], other))
    for hop in crossing:
        hop.wait_recv()

    trace = jnp.zeros((), F32)
    eye = lax.broadcasted_iota(jnp.int32, (128, 128), 0) == lax.broadcasted_iota(jnp.int32, (128, 128), 1)
    for h in range(2):
        rows_a = ga[h, :, :, c].reshape(16 * BA, 128)
        rows_b = gb[h, :, :, c].reshape(16 * BB, 128)
        for b in range(BLOCKS):
            if b < 9:
                i = 3 * h + b // 3
                j = (i + b % 3) % 6
            else:
                i = 2 * h + b - 9
                j = (i + 3) % 6
            if i == 3 and j == 0:
                continue
            block = rows_a[b * 128 : (b + 1) * 128] if b < 6 else rows_b[(b - 6) * 128 : (b - 5) * 128]
            g[i * 128 : (i + 1) * 128, j * 128 : (j + 1) * 128] = block
            if i == j:
                trace = trace + jnp.sum(jnp.where(eye, block, 0.0))
            else:
                g[j * 128 : (j + 1) * 128, i * 128 : (i + 1) * 128] = block.T
    inverse = 1.0 / (jnp.sqrt(jnp.broadcast_to(trace, (8, 128))) + NORM_EPSILON)
    scale = inverse[0:1, 0:1]
    square = scale * scale
    for j in range(3):
        put(ah, al, slice(0, R), COLS[j], g[:, COLS[j]] * square)
    corner = lax.broadcasted_iota(jnp.int32, (256, 256), 0) == lax.broadcasted_iota(jnp.int32, (256, 256), 1)
    linear = jnp.where(corner, QUINTIC_LINEAR, 0.0)

    def polynomial(value, i, j):
        value = (QUINTIC_CUBIC * square) * g[COLS[i], COLS[j]] + QUINTIC_FIFTH * value
        return linear + value if i == j else value

    symmetric_product((ah, al), (ah, al), (ph, plo), polynomial)

    symmetric_product((ph, plo), (ah, al), (bh, bl))
    symmetric_product((ph, plo), (bh, bl), (ah, al))

    handed.wait_recv()
    factor = UPDATE_FACTOR * math.sqrt(max(D, R))
    halves = (slice(224, 448), slice(0, 224))
    every = slice(0, R)
    put(wh, wl, halves[1], every, dall[pl.ds(4 * c, 4)].reshape(224, R))
    put(wh, wl, halves[0], every, dother[...].reshape(224, R))
    for rows in halves:
        x1 = dot3((wh[rows, :], wl[rows, :]), (ph[...], plo[...])) * scale
        work[rows, :] = QUINTIC_LINEAR * x1
        put(xh, xl, rows, every, x1)
    for rows in halves:
        y1 = dot3((xh[rows, :], xl[rows, :]), (ah[...], al[...]))
        work[rows, :] = work[rows, :] + QUINTIC_CUBIC * y1
        put(wh, wl, rows, every, y1)

    def finish(rows):
        return factor * (work[rows, :] + QUINTIC_FIFTH * dot3((wh[rows, :], wl[rows, :]), (ah[...], al[...])))

    theirs[...] = finish(halves[0])
    back = go(remote(theirs, up_ref.at[c], usem.at[0], usem.at[1], other))
    up_ref[c] = finish(halves[1])
    back.wait_recv()
    for copy in started:
        copy.wait_send()
    for condition, copy in local:
        pl.when(condition)(copy.wait_send)


def dot3(left, right):
    (lh, ll), (rh, rl) = left, right

    def dot(a, b):
        return jnp.dot(a, b, preferred_element_type=F32)

    return dot(lh, rh) + (dot(lh, rl) + dot(ll, rh))


def put(hi_ref, lo_ref, rows, cols, value):
    hi = value.astype(BF16)
    hi_ref[rows, cols] = hi
    lo_ref[rows, cols] = (value - hi.astype(F32)).astype(BF16)


COLS = [slice(j * 256, (j + 1) * 256) for j in range(3)]


def symmetric_product(left, right, out, then=None):
    (lh, ll), (rh, rl) = left, right
    for j in range(3):
        rows = slice(0, (j + 1) * 256)
        block = dot3((lh[rows, :], ll[rows, :]), (rh[:, COLS[j]], rl[:, COLS[j]]))
        for i in range(j + 1):
            value = block[COLS[i]]
            if then is not None:
                value = then(value, i, j)
            put(*out, COLS[i], COLS[j], value)
            if i < j:
                put(*out, COLS[j], COLS[i], value.T)


def update_kernel(nm_ref, up_ref, w_ref, nm_out, up_out, nw_out, nw, sems):
    copies = [pltpu.make_async_copy(nm_ref, nm_out, sems.at[0]), pltpu.make_async_copy(up_ref, up_out, sems.at[1])]
    for copy in copies:
        copy.start()
    for i in range(4):
        rows = pl.ds(i * 112, 112)
        weights = w_ref[rows, :]
        nw[rows, :] = weights - LEARNING_RATE * (up_ref[rows, :] + WEIGHT_DECAY * weights)
        copies.append(pltpu.make_async_copy(nw.at[rows], nw_out.at[rows], sems.at[2 + i]))
        copies[-1].start()
    for copy in copies:
        copy.wait()


def shards(replica_grads, momentum, weights):
    grads = pltpu.with_memory_space_constraint(replica_grads.reshape(NZ * CH, R), pltpu.HBM)
    momentum = pltpu.with_memory_space_constraint(momentum.reshape(NZ, CH, R), pltpu.HBM)
    weights = weights.reshape(NZ * CH, R)
    vmem = pl.BlockSpec(memory_space=pltpu.VMEM)
    hbm = pl.BlockSpec(memory_space=pltpu.HBM)
    sem = pltpu.SemaphoreType.DMA
    rows = pltpu.VMEM((NZ * CH, R), BF16)
    half = pltpu.VMEM((R, R), BF16)
    new_momentum, update = pl.pallas_call(
        gram_kernel,
        out_shape=(
            jax.ShapeDtypeStruct((NZ, CH, R), F32),
            jax.ShapeDtypeStruct((2, 224, R), F32),
        ),
        in_specs=[hbm, hbm],
        out_specs=(vmem, vmem),
        scratch_shapes=[
            pltpu.VMEM((NZ * CH, R), BF16),
            pltpu.VMEM((NZ, CH, R), F32),
            pltpu.VMEM((2, 4, 4, 2, BA, 128), F32),
            pltpu.VMEM((2, 4, 4, 2, BB, 128), F32),
            pltpu.VMEM((R, R), F32), half, half, half, half, half, half, rows, rows, rows, rows,
            pltpu.VMEM((NZ * CH, R), F32),
            pltpu.VMEM((224, R), F32),
            pltpu.VMEM((NZ, CH, R), F32),
            pltpu.VMEM((4, CH, R), F32),
            pltpu.VMEM((NZ, CH, R), F32),
            pltpu.VMEM((4, CH, R), F32),
            pltpu.VMEM((3, CH, R), F32),
            pltpu.VMEM((NZ, CH, R), F32),
            pltpu.VMEM((2 * CH, R), F32),
            pltpu.VMEM((2 * CH, R + W), BF16),
            pltpu.VMEM((2 * CH, R + W), BF16),
            pltpu.VMEM((BLOCKS * 128, 128), F32),
            pltpu.VMEM((3, 4 * BA, 128), F32),
            pltpu.VMEM((3, 4 * BB, 128), F32),
            pltpu.VMEM((2, 4, 48, 128), F32),
            pltpu.VMEM((16, 24, 128), F32),
            pltpu.VMEM((24, 128), F32),
            pltpu.VMEM((2, 96, 128), F32),
            sem,
            sem,
        ]
        + [sem((4, SUB)), sem((4, SUB)), sem((3, SUB)), sem((3, SUB))] * 2
        + [sem((SUB,))] * 2
        + [sem((3,))] * 4
        + [sem((2, 4, 2)), sem((4, 4))]
        + [sem((8,))] * 2
        + [sem((2, 3))] * 4
        + [sem((2, 3, 4))] * 4
        + [sem((2, 4))] * 2
        + [sem((2,))] * 2
        + [pltpu.SemaphoreType.REGULAR] * 2,
        compiler_params=pltpu.CompilerParams(collective_id=0, has_side_effects=True, vmem_limit_bytes=34 << 20),
        name="gram",
    )(grads, momentum)
    like = jax.ShapeDtypeStruct((NZ * CH, R), F32)
    outs = pl.pallas_call(
        update_kernel,
        out_shape=(like, like, like),
        in_specs=[vmem] * 3,
        out_specs=(hbm, hbm, hbm),
        scratch_shapes=[pltpu.VMEM((NZ * CH, R), F32), sem((6,))],
        compiler_params=pltpu.CompilerParams(vmem_limit_bytes=4 << 20),
        name="update",
    )(new_momentum.reshape(NZ * CH, R), update.reshape(NZ * CH, R), weights)
    return tuple(o.reshape(2, 224, R) for o in outs)


def solution(mesh):
    return jax.shard_map(
        shards,
        mesh=mesh,
        in_specs=(P("dp", None, "fsdp", None), P(None, "fsdp", None), P(None, "fsdp", None)),
        out_specs=(P(None, "fsdp", None), P(None, "fsdp", None), P(None, "fsdp", None)),
        check_vma=False,
    )
```

```python
import functools
import math

import jax
import jax.numpy as jnp
from jax import lax
from jax.experimental import pallas as pl
from jax.experimental.pallas import tpu as pltpu
from jax.sharding import PartitionSpec as P

D = 7168
R = 768

QUINTIC_LINEAR = 3.4445
QUINTIC_CUBIC = -4.775
QUINTIC_FIFTH = 2.0315
MOMENTUM_FACTOR = 0.95
LEARNING_RATE = 0.02
WEIGHT_DECAY = 0.1
NORM_EPSILON = 1e-07
UPDATE_FACTOR = 0.2

MESH = pl.DeviceIdType.MESH
F32 = jnp.float32
BF16 = jnp.bfloat16
NZ = 8
CH = 56
SUB = 3
W = R // SUB
BA, BB = 40, 32
BLOCKS = 9
SPLIT = 16 * BA


def device(x, y, z, c):
    return (z, (x * 4 + y) * 2 + c)


def remote(src, dst, send, recv, target):
    return pltpu.make_async_remote_copy(
        src_ref=src, dst_ref=dst, send_sem=send, recv_sem=recv, device_id=target, device_id_type=MESH
    )


def gram_kernel(
    g_ref, m_ref, nm_ref, up_ref,
    graw, s_ref, ga, gb, g, ah, al, ph, plo, bh, bl, wh, wl, xh, xl, work, theirs, dall, dother,
    acc, rl, rs, mbuf, dx, dh, dl, packed, tile, rt, ra1, rb1, half, rz, piece, gz,
    msem, gsem, ls, lr, ss, sr, als, alr, ass, asr, cs, cr,
    a1s, a1r, b1s, b1r, ts, tr, ms, mr, z2s, z2r,
    ga1s, ga1r, gb1s, gb1r, ga2s, ga2r, gb2s, gb2r, dsem, usem, ready, summed,
):
    z = lax.axis_index("dp")
    f = lax.axis_index("fsdp")
    c = f % 2
    y = (f // 2) % 4
    x = f // 8
    layer = z // 4
    q = z % 4
    other = device(x, y, z, 1 - c)
    way = 1 - 2 * c
    up = device(x, y, (z + way + NZ) % NZ, c)
    down = device(x, y, (z - way + NZ) % NZ, c)

    def chunk(offset):
        return (z + way * offset + 2 * NZ) % NZ

    load = pltpu.make_async_copy(g_ref, graw, gsem)
    load.start()
    fetch = pltpu.make_async_copy(m_ref, mbuf, msem)
    fetch.start()

    barrier = pltpu.get_barrier_semaphore()
    greeted = [other]
    greeted += [device(x, y, (z + o) % NZ, c) for o in (1, NZ - 1)]
    beside = [device((x + o) % 4, y, z, c) for o in (1, 3)] + [device(x, (y + o) % 4, z, c) for o in (1, 3)]
    greeted += beside
    for target in greeted:
        pl.semaphore_signal(barrier, inc=1, device_id=target, device_id_type=MESH)
    load.wait()
    for i in range(4):
        rows = graw[i * 2 * CH : (i + 1) * 2 * CH, :].astype(F32)
        acc[2 * i] = rows[:CH]
        acc[2 * i + 1] = rows[CH:]
    pl.semaphore_wait(barrier, len(greeted))
    for target in beside:
        pl.semaphore_signal(ready, inc=1, device_id=target, device_id_type=MESH)

    def cols(k):
        return pl.ds(k * W, W)

    started = []
    local = []

    def go(copy):
        copy.start()
        started.append(copy)
        return copy

    def long_hop(step, k):
        return remote(acc.at[chunk(4 - step), :, cols(k)], rl.at[step, :, cols(k)], ls.at[step, k], lr.at[step, k], up)

    def short_hop(step, k):
        return remote(acc.at[chunk(step - 3), :, cols(k)], rs.at[step, :, cols(k)], ss.at[step, k], sr.at[step, k], down)

    hops = {}
    for k in range(SUB):
        hops["l", 0, k] = go(long_hop(0, k))
        hops["s", 0, k] = go(short_hop(0, k))
    for step in range(1, 4):
        for k in range(SUB):
            hops["l", step - 1, k].wait_recv()
            at = chunk(4 - step)
            acc[at, :, cols(k)] = acc[at, :, cols(k)] + rl[step - 1, :, cols(k)]
            hops["l", step, k] = go(long_hop(step, k))
            if step < 3:
                hops["s", step - 1, k].wait_recv()
                at = chunk(step - 3)
                acc[at, :, cols(k)] = acc[at, :, cols(k)] + rs[step - 1, :, cols(k)]
                hops["s", step, k] = go(short_hop(step, k))

    def gather_up(step, k):
        at = chunk(-step)
        return remote(s_ref.at[at, :, cols(k)], s_ref.at[at, :, cols(k)], als.at[step, k], alr.at[step, k], up)

    def gather_down(step, k):
        at = chunk(step)
        return remote(s_ref.at[at, :, cols(k)], s_ref.at[at, :, cols(k)], ass.at[step, k], asr.at[step, k], down)

    fetch.wait()
    mine = []
    for k in range(SUB):
        hops["s", 2, k].wait_recv()
        hops["l", 3, k].wait_recv()
        total = acc[z, :, cols(k)] + rs[2, :, cols(k)] + rl[3, :, cols(k)]
        s_ref[z, :, cols(k)] = total
        d = total + MOMENTUM_FACTOR * (MOMENTUM_FACTOR * mbuf[z, :, cols(k)] + total)
        dx[0:CH, cols(k)] = d
        mine.append(
            go(remote(dx.at[pl.ds(0, CH), cols(k)], dx.at[pl.ds(CH, CH), cols(k)], cs.at[k], cr.at[k], other))
        )
        hops["u", 0, k] = go(gather_up(0, k))
        hops["d", 0, k] = go(gather_down(0, k))

    pl.semaphore_wait(ready, len(beside))
    around = [device((x + o) % 4, y, z, c) for o in (1, 2, 3)] + [device(x, (y + o) % 4, z, c) for o in (1, 2, 3)]
    for target in around:
        pl.semaphore_signal(summed, inc=1, device_id=target, device_id_type=MESH)

    for k in range(SUB):
        mine[k].wait_recv()
        d = dx[:, cols(k)]
        hi = d.astype(BF16)
        lo = (d - hi.astype(F32)).astype(BF16)
        dh[:, cols(k)] = hi
        dl[:, cols(k)] = lo
        if k == 0:
            dh[:, R : R + W] = hi
            dl[:, R : R + W] = lo

    ROW = lax.broadcasted_iota(jnp.int32, (128, 128), 0)
    COL = lax.broadcasted_iota(jnp.int32, (128, 128), 1)

    def gram(first, second, width):
        li = pl.ds(pl.multiple_of(first * 128, 128), 128)
        ri = pl.ds(pl.multiple_of(second * 128, 128), width)

        def dot(left, right):
            return lax.dot_general(left, right, (((0,), (0,)), ((), ())), preferred_element_type=F32)

        lh, ll, rh, rlo = dh[:, li], dl[:, li], dh[:, ri], dl[:, ri]
        return dot(lh, rh) + (dot(lh, rlo) + dot(ll, rh))

    for a in range(3):
        block = gram(3 * c + a, 3 * c + a + 1, 256)
        packed[2 * a * 128 : (2 * a + 1) * 128, :] = block[:, :128]
        packed[(2 * a + 1) * 128 : (2 * a + 2) * 128, :] = block[:, 128:]

    def corner_blocks():
        @pl.when(c == 0)
        def _():
            for e in range(3):
                packed[(6 + e) * 128 : (7 + e) * 128, :] = gram(e, e + 3, 128)

        @pl.when(c == 1)
        def _():
            upper = ROW <= COL
            for e in range(3):
                packed[(6 + e) * 128 : (7 + e) * 128, :] = jnp.where(upper, gram(e, e, 128), gram(e + 3, e + 3, 128))

    pa = (x * (1 - c) + y * c, y * (1 - c) + x * c)
    pb = (pa[1], pa[0])

    def on_a(first, second, plane):
        return device(first * (1 - c) + second * c, second * (1 - c) + first * c, plane, c)

    def on_b(first, second, plane):
        return on_a(second, first, plane)

    paths = (
        (0, BA, pa, on_a, ra1, a1s, a1r, ga, ga1s, ga1r, ga2s, ga2r),
        (SPLIT, BB, pb, on_b, rb1, b1s, b1r, gb, gb1s, gb1r, gb2s, gb2r),
    )
    order = (2, 1, 3)

    first_hops = []

    def start_first(base, rows, at, on, r1, s1, t1, *_):
        size = 4 * rows
        for o in order:
            to = (at[0] + o) % 4
            src = packed.at[pl.ds(pl.multiple_of(base + to * size, 8), size)]
            first_hops.append(go(remote(src, r1.at[o - 1], s1.at[o - 1], t1.at[o - 1], on(to, at[1], z))))

    start_first(*paths[0])
    corner_blocks()
    start_first(*paths[1])
    tile[...] = jnp.zeros((8, 128), F32)
    for e in range(3):
        d = dx[:, (e + 3) * 128 : (e + 4) * 128]
        tile[e : e + 1, :] = jnp.sum(d * d, axis=0, keepdims=True)
    tiles = [go(remote(tile, rt.at[o - 1], ts.at[o - 1], tr.at[o - 1], on_a((pa[0] + o) % 4, pa[1], z))) for o in order]

    def settle(offset):
        at = chunk(offset)
        nm_ref[at] = MOMENTUM_FACTOR * mbuf[at] + s_ref[at]
        dall[at] = s_ref[at] + MOMENTUM_FACTOR * nm_ref[at]

    settle(0)
    for k in range(SUB):
        hops["u", 0, k].wait_recv()
        hops["u", 1, k] = go(gather_up(1, k))
        hops["d", 0, k].wait_recv()
        hops["d", 1, k] = go(gather_down(1, k))

    pl.semaphore_wait(summed, len(around))
    for n, (base, rows, (p1, p2), on, r1, *_) in enumerate(paths):
        size = 4 * rows
        for hop in first_hops[3 * n : 3 * n + 3]:
            hop.wait_recv()
        own = pl.ds(pl.multiple_of(base + p1 * size, 8), size)
        total = (packed[own, :] + r1[0]) + (r1[1] + r1[2])
        if n == 0:
            for hop in tiles:
                hop.wait_recv()
            squares = (tile[...] + rt[0]) + (rt[1] + rt[2])
        for i in range(4):
            if n == 0:
                half[0, i, :BA] = total[i * BA : (i + 1) * BA]
                half[0, i, BA:] = squares
            else:
                half[1, i, 0:16] = total[i * BB : i * BB + 16]
                half[1, i, 16:24] = squares
                half[1, i, 24:40] = total[i * BB + 16 : (i + 1) * BB]
                half[1, i, 40:48] = squares
        for o in (2, 1, 3, 0):
            to = (p2 + o) % 4
            for h in range(2):
                plane = 2 * n + h
                copy = remote(
                    half.at[n, to, pl.ds(24 * h, 24)], rz.at[4 * o + q], ms.at[n, o, h], mr.at[o, q],
                    on(p1, to, 4 * layer + plane),
                )
                if o > 0:
                    go(copy)
                else:
                    pl.when(q != plane)(copy.start)
                    local.append((q != plane, copy))
    settle(1)
    settle(-1)
    mine_n, mine_h = q // 2, q % 2
    mine_2 = pa[1] * (1 - mine_n) + pb[1] * mine_n
    rz[q] = half[mine_n, mine_2, pl.ds(pl.multiple_of(24 * mine_h, 8), 24)]
    for o in range(4):
        for plane in range(4):
            copy = remote(piece, rz.at[4 * o + plane], ms.at[0, 0, 0], mr.at[o, plane], other)
            if o > 0:
                copy.wait_recv()
            else:
                pl.when(q != plane)(copy.wait_recv)
    sums = [rz[i] for i in range(16)]
    while len(sums) > 1:
        sums = [sums[2 * i] + sums[2 * i + 1] for i in range(len(sums) // 2)]
    at = pl.ds(pl.multiple_of(q * 24, 8), 24)
    piece[...] = sums[0]
    for o in (4, 3, 5, 2, 6, 1, 7):
        go(remote(piece, gz.at[c, at], z2s.at[o], z2r.at[c, q], device(x, y, (z + o) % NZ, layer)))

    @pl.when(layer == c)
    def _():
        gz[c, at, :] = piece[...]

    copy = remote(piece, gz.at[c, at], z2s.at[0], z2r.at[c, q], other)
    pl.when(layer != c)(copy.start)
    local.append((layer != c, copy))

    near, far = {}, {}

    def start_far(n, j):
        base, rows, (p1, p2), on, r1, s1, t1, out, u1, v1, u2, v2 = paths[n]
        block = out.at[p1, (p2 + 4 - j) % 4]
        for o in order:
            far[n, o, j] = go(remote(block, block, u2.at[o - 1, j], v2.at[o - 1, j], on((p1 + o) % 4, p2, z)))

    for n, (base, rows, (p1, p2), on, r1, s1, t1, out, u1, v1, u2, v2) in enumerate(paths):
        for quarter in (2 * n, 2 * n + 1):
            for h in range(2):
                arrival = remote(piece, gz.at[h, pl.ds(24 * quarter, 24)], z2s.at[0], z2r.at[h, quarter], other)
                pl.when((layer != c) | (c != h) | (q != quarter))(arrival.wait_recv)
        if n == 0:
            out[p1, p2] = gz[:, 0:BA, :]
        else:
            out[p1, p2, :, 0:16] = gz[:, 48:64, :]
            out[p1, p2, :, 16:32] = gz[:, 72:88, :]
        block = out.at[p1, p2]
        for o in order:
            near[n, o] = go(remote(block, block, u1.at[o - 1], v1.at[o - 1], on(p1, (p2 + o) % 4, z)))
    for n in range(2):
        start_far(n, 0)

    for k in range(SUB):
        hops["u", 1, k].wait_recv()
        hops["u", 2, k] = go(gather_up(2, k))
        hops["d", 1, k].wait_recv()
        hops["d", 2, k] = go(gather_down(2, k))
    settle(2)
    settle(-2)

    for o in order:
        for n in range(2):
            near[n, o].wait_recv()
            start_far(n, o)

    for k in range(SUB):
        hops["u", 2, k].wait_recv()
        hops["u", 3, k] = go(gather_up(3, k))
    for k in range(SUB):
        hops["d", 2, k].wait_recv()
    settle(-3)
    settle(3)

    for k in range(SUB):
        hops["u", 3, k].wait_recv()
    settle(-4)
    handed = go(remote(dall.at[pl.ds(4 * (1 - c), 4)], dother, dsem.at[0], dsem.at[1], other))
    for hop in far.values():
        hop.wait_recv()

    diagonals = gz[0, BA : BA + 8, :]
    trace = jnp.sum(diagonals)

    def place(i, j, block):
        g[i * 128 : (i + 1) * 128, j * 128 : (j + 1) * 128] = block

    for h in range(2):
        turned = h + c - 2 * h * c
        places = [(i * (1 - turned) + j * turned, j * (1 - turned) + i * turned) for i in range(4) for j in range(4)]
        rows_a = jnp.concatenate([ga[i, j, h] for i, j in places], axis=0)
        rows_b = jnp.concatenate([gb[i, j, h] for i, j in places], axis=0)
        for b in range(BLOCKS):
            block = rows_a[b * 128 : (b + 1) * 128] if b < 5 else rows_b[(b - 5) * 128 : (b - 4) * 128]
            if b < 6:
                i = 3 * h + b // 2
                j = (i + 1 + b % 2) % 6
            else:
                i, j = b - 6, b - 3
            if b < 6 or h == 0:
                place(i, j, block)
                place(j, i, block.T)
            else:
                trace = trace + jnp.sum(jnp.where(ROW == COL, block, 0.0))
                above = jnp.where(ROW < COL, block, 0.0)
                below = jnp.where(ROW > COL, block, 0.0)
                place(i, i, jnp.where(ROW <= COL, block, 0.0) + above.T)
                place(j, j, below + below.T + jnp.where(ROW == COL, diagonals[i : i + 1, :], 0.0))
    inverse = 1.0 / (jnp.sqrt(jnp.broadcast_to(trace, (8, 128))) + NORM_EPSILON)
    scale = inverse[0:1, 0:1]
    square = scale * scale
    for j in range(3):
        put(ah, al, slice(0, R), COLS[j], g[:, COLS[j]] * square)
    corner = lax.broadcasted_iota(jnp.int32, (256, 256), 0) == lax.broadcasted_iota(jnp.int32, (256, 256), 1)
    linear = jnp.where(corner, QUINTIC_LINEAR, 0.0)

    def polynomial(value, i, j):
        value = (QUINTIC_CUBIC * square) * g[COLS[i], COLS[j]] + QUINTIC_FIFTH * value
        return linear + value if i == j else value

    symmetric_product((ah, al), (ah, al), (ph, plo), polynomial)

    symmetric_product((ph, plo), (ah, al), (bh, bl))
    symmetric_product((ph, plo), (bh, bl), (ah, al))

    handed.wait_recv()
    factor = UPDATE_FACTOR * math.sqrt(max(D, R))
    halves = (slice(224, 448), slice(0, 224))
    every = slice(0, R)
    put(wh, wl, halves[1], every, dall[pl.ds(4 * c, 4)].reshape(224, R))
    put(wh, wl, halves[0], every, dother[...].reshape(224, R))
    for rows in halves:
        x1 = dot3((wh[rows, :], wl[rows, :]), (ph[...], plo[...])) * scale
        work[rows, :] = QUINTIC_LINEAR * x1
        put(xh, xl, rows, every, x1)
    for rows in halves:
        y1 = dot3((xh[rows, :], xl[rows, :]), (ah[...], al[...]))
        work[rows, :] = work[rows, :] + QUINTIC_CUBIC * y1
        put(wh, wl, rows, every, y1)

    def finish(rows):
        return factor * (work[rows, :] + QUINTIC_FIFTH * dot3((wh[rows, :], wl[rows, :]), (ah[...], al[...])))

    theirs[...] = finish(halves[0])
    back = go(remote(theirs, up_ref.at[c], usem.at[0], usem.at[1], other))
    up_ref[c] = finish(halves[1])
    back.wait_recv()
    for copy in started:
        copy.wait_send()
    for condition, copy in local:
        pl.when(condition)(copy.wait_send)


def dot3(left, right):
    (lh, ll), (rh, rl) = left, right

    def dot(a, b):
        return jnp.dot(a, b, preferred_element_type=F32)

    return dot(lh, rh) + (dot(lh, rl) + dot(ll, rh))


def put(hi_ref, lo_ref, rows, cols, value):
    hi = value.astype(BF16)
    hi_ref[rows, cols] = hi
    lo_ref[rows, cols] = (value - hi.astype(F32)).astype(BF16)


COLS = [slice(j * 256, (j + 1) * 256) for j in range(3)]


def symmetric_product(left, right, out, then=None):
    (lh, ll), (rh, rl) = left, right
    for j in range(3):
        rows = slice(0, (j + 1) * 256)
        block = dot3((lh[rows, :], ll[rows, :]), (rh[:, COLS[j]], rl[:, COLS[j]]))
        for i in range(j + 1):
            value = block[COLS[i]]
            if then is not None:
                value = then(value, i, j)
            put(*out, COLS[i], COLS[j], value)
            if i < j:
                put(*out, COLS[j], COLS[i], value.T)


def update_kernel(nm_ref, up_ref, w_ref, nm_out, up_out, nw_out, nw, sems):
    copies = [pltpu.make_async_copy(nm_ref, nm_out, sems.at[0]), pltpu.make_async_copy(up_ref, up_out, sems.at[1])]
    for copy in copies:
        copy.start()
    for i in range(4):
        rows = pl.ds(i * 112, 112)
        weights = w_ref[rows, :]
        nw[rows, :] = weights - LEARNING_RATE * (up_ref[rows, :] + WEIGHT_DECAY * weights)
        copies.append(pltpu.make_async_copy(nw.at[rows], nw_out.at[rows], sems.at[2 + i]))
        copies[-1].start()
    for copy in copies:
        copy.wait()


def shards(replica_grads, momentum, weights):
    grads = pltpu.with_memory_space_constraint(replica_grads.reshape(NZ * CH, R), pltpu.HBM)
    momentum = pltpu.with_memory_space_constraint(momentum.reshape(NZ, CH, R), pltpu.HBM)
    weights = weights.reshape(NZ * CH, R)
    vmem = pl.BlockSpec(memory_space=pltpu.VMEM)
    hbm = pl.BlockSpec(memory_space=pltpu.HBM)
    sem = pltpu.SemaphoreType.DMA
    rows = pltpu.VMEM((NZ * CH, R), BF16)
    half = pltpu.VMEM((R, R), BF16)
    new_momentum, update = pl.pallas_call(
        gram_kernel,
        out_shape=(
            jax.ShapeDtypeStruct((NZ, CH, R), F32),
            jax.ShapeDtypeStruct((2, 224, R), F32),
        ),
        in_specs=[hbm, hbm],
        out_specs=(vmem, vmem),
        scratch_shapes=[
            pltpu.VMEM((NZ * CH, R), BF16),
            pltpu.VMEM((NZ, CH, R), F32),
            pltpu.VMEM((4, 4, 2, BA, 128), F32),
            pltpu.VMEM((4, 4, 2, BB, 128), F32),
            pltpu.VMEM((R, R), F32), half, half, half, half, half, half, rows, rows, rows, rows,
            pltpu.VMEM((NZ * CH, R), F32),
            pltpu.VMEM((224, R), F32),
            pltpu.VMEM((NZ, CH, R), F32),
            pltpu.VMEM((4, CH, R), F32),
            pltpu.VMEM((NZ, CH, R), F32),
            pltpu.VMEM((4, CH, R), F32),
            pltpu.VMEM((3, CH, R), F32),
            pltpu.VMEM((NZ, CH, R), F32),
            pltpu.VMEM((2 * CH, R), F32),
            pltpu.VMEM((2 * CH, R + W), BF16),
            pltpu.VMEM((2 * CH, R + W), BF16),
            pltpu.VMEM((BLOCKS * 128, 128), F32),
            pltpu.VMEM((8, 128), F32),
            pltpu.VMEM((3, 8, 128), F32),
            pltpu.VMEM((3, 4 * BA, 128), F32),
            pltpu.VMEM((3, 4 * BB, 128), F32),
            pltpu.VMEM((2, 4, 48, 128), F32),
            pltpu.VMEM((16, 24, 128), F32),
            pltpu.VMEM((24, 128), F32),
            pltpu.VMEM((2, 96, 128), F32),
            sem,
            sem,
        ]
        + [sem((4, SUB)), sem((4, SUB)), sem((3, SUB)), sem((3, SUB))] * 2
        + [sem((SUB,))] * 2
        + [sem((3,))] * 6
        + [sem((2, 4, 2)), sem((4, 4))]
        + [sem((8,)), sem((2, 4))]
        + [sem((3,))] * 4
        + [sem((3, 4))] * 4
        + [sem((2,))] * 2
        + [pltpu.SemaphoreType.REGULAR] * 2,
        compiler_params=pltpu.CompilerParams(collective_id=0, has_side_effects=True, vmem_limit_bytes=34 << 20),
        name="gram",
    )(grads, momentum)
    like = jax.ShapeDtypeStruct((NZ * CH, R), F32)
    outs = pl.pallas_call(
        update_kernel,
        out_shape=(like, like, like),
        in_specs=[vmem] * 3,
        out_specs=(hbm, hbm, hbm),
        scratch_shapes=[pltpu.VMEM((NZ * CH, R), F32), sem((6,))],
        compiler_params=pltpu.CompilerParams(vmem_limit_bytes=4 << 20),
        name="update",
    )(new_momentum.reshape(NZ * CH, R), update.reshape(NZ * CH, R), weights)
    return tuple(o.reshape(2, 224, R) for o in outs)


def solution(mesh):
    return jax.shard_map(
        shards,
        mesh=mesh,
        in_specs=(P("dp", None, "fsdp", None), P(None, "fsdp", None), P(None, "fsdp", None)),
        out_specs=(P(None, "fsdp", None), P(None, "fsdp", None), P(None, "fsdp", None)),
        check_vma=False,
    )
```

```python
import functools
import math

import jax
import jax.numpy as jnp
from jax import lax
from jax.experimental import pallas as pl
from jax.experimental.pallas import tpu as pltpu
from jax.sharding import PartitionSpec as P

D = 7168
R = 768

QUINTIC_LINEAR = 3.4445
QUINTIC_CUBIC = -4.775
QUINTIC_FIFTH = 2.0315
MOMENTUM_FACTOR = 0.95
LEARNING_RATE = 0.02
WEIGHT_DECAY = 0.1
NORM_EPSILON = 1e-07
UPDATE_FACTOR = 0.2

MESH = pl.DeviceIdType.MESH
F32 = jnp.float32
BF16 = jnp.bfloat16
NZ = 8
CH = 56
SUB = 3
W = R // SUB
BA, BB = 40, 32
BLOCKS = 9
SPLIT = 16 * BA


def device(x, y, z, c):
    return (z, (x * 4 + y) * 2 + c)


def remote(src, dst, send, recv, target):
    return pltpu.make_async_remote_copy(
        src_ref=src, dst_ref=dst, send_sem=send, recv_sem=recv, device_id=target, device_id_type=MESH
    )


def gram_kernel(
    g_ref, m_ref, nm_ref, up_ref,
    graw, s_ref, ga, gb, g, ah, al, ph, plo, bh, bl, wh, wl, xh, xl, work, theirs, dall, dother,
    acc, rl, rs, mbuf, dx, dh, dl, packed, tile, rt, ra1, rb1, half, rz, piece, gz,
    msem, gsem, ls, lr, ss, sr, als, alr, ass, asr, cs, cr,
    a1s, a1r, b1s, b1r, ts, tr, ms, mr, z2s, z2r,
    ga1s, ga1r, gb1s, gb1r, ga2s, ga2r, gb2s, gb2r, dsem, usem, ready, summed,
):
    z = lax.axis_index("dp")
    f = lax.axis_index("fsdp")
    c = f % 2
    y = (f // 2) % 4
    x = f // 8
    layer = z // 4
    q = z % 4
    other = device(x, y, z, 1 - c)
    way = 1 - 2 * c
    up = device(x, y, (z + way + NZ) % NZ, c)
    down = device(x, y, (z - way + NZ) % NZ, c)

    def chunk(offset):
        return (z + way * offset + 2 * NZ) % NZ

    load = pltpu.make_async_copy(g_ref, graw, gsem)
    load.start()
    fetch = pltpu.make_async_copy(m_ref, mbuf, msem)
    fetch.start()

    barrier = pltpu.get_barrier_semaphore()
    greeted = [other]
    greeted += [device(x, y, (z + o) % NZ, c) for o in (1, NZ - 1)]
    beside = [device((x + o) % 4, y, z, c) for o in (1, 3)] + [device(x, (y + o) % 4, z, c) for o in (1, 3)]
    greeted += beside
    for target in greeted:
        pl.semaphore_signal(barrier, inc=1, device_id=target, device_id_type=MESH)
    load.wait()
    for i in range(4):
        rows = graw[i * 2 * CH : (i + 1) * 2 * CH, :].astype(F32)
        acc[2 * i] = rows[:CH]
        acc[2 * i + 1] = rows[CH:]
    pl.semaphore_wait(barrier, len(greeted))
    for target in beside:
        pl.semaphore_signal(ready, inc=1, device_id=target, device_id_type=MESH)

    def cols(k):
        return pl.ds(k * W, W)

    started = []
    local = []

    def go(copy):
        copy.start()
        started.append(copy)
        return copy

    def drain():
        for copy in started:
            copy.wait_send()
        for condition, copy in local:
            pl.when(condition)(copy.wait_send)
        started.clear()
        local.clear()

    def long_hop(step, k):
        return remote(acc.at[chunk(4 - step), :, cols(k)], rl.at[step, :, cols(k)], ls.at[step, k], lr.at[step, k], up)

    def short_hop(step, k):
        return remote(acc.at[chunk(step - 3), :, cols(k)], rs.at[step, :, cols(k)], ss.at[step, k], sr.at[step, k], down)

    hops = {}
    for k in range(SUB):
        hops["l", 0, k] = go(long_hop(0, k))
        hops["s", 0, k] = go(short_hop(0, k))
    for step in range(1, 4):
        for k in range(SUB):
            hops["l", step - 1, k].wait_recv()
            at = chunk(4 - step)
            acc[at, :, cols(k)] = acc[at, :, cols(k)] + rl[step - 1, :, cols(k)]
            hops["l", step, k] = go(long_hop(step, k))
            if step < 3:
                hops["s", step - 1, k].wait_recv()
                at = chunk(step - 3)
                acc[at, :, cols(k)] = acc[at, :, cols(k)] + rs[step - 1, :, cols(k)]
                hops["s", step, k] = go(short_hop(step, k))

    def gather_up(step):
        block = s_ref.at[chunk(-step)]
        hops["u", step] = go(remote(block, block, als.at[step], alr.at[step], up))

    def gather_down(step):
        block = s_ref.at[chunk(step)]
        hops["d", step] = go(remote(block, block, ass.at[step], asr.at[step], down))

    fetch.wait()
    mine = []
    for k in range(SUB):
        hops["s", 2, k].wait_recv()
        hops["l", 3, k].wait_recv()
        total = acc[z, :, cols(k)] + rs[2, :, cols(k)] + rl[3, :, cols(k)]
        s_ref[z, :, cols(k)] = total
        d = total + MOMENTUM_FACTOR * (MOMENTUM_FACTOR * mbuf[z, :, cols(k)] + total)
        dx[0:CH, cols(k)] = d
        mine.append(
            go(remote(dx.at[pl.ds(0, CH), cols(k)], dx.at[pl.ds(CH, CH), cols(k)], cs.at[k], cr.at[k], other))
        )
    gather_up(0)
    gather_down(0)

    pl.semaphore_wait(ready, len(beside))
    around = [device((x + o) % 4, y, z, c) for o in (1, 2, 3)] + [device(x, (y + o) % 4, z, c) for o in (1, 2, 3)]
    for target in around:
        pl.semaphore_signal(summed, inc=1, device_id=target, device_id_type=MESH)

    for k in range(SUB):
        mine[k].wait_recv()
        d = dx[:, cols(k)]
        hi = d.astype(BF16)
        lo = (d - hi.astype(F32)).astype(BF16)
        dh[:, cols(k)] = hi
        dl[:, cols(k)] = lo
        if k == 0:
            dh[:, R : R + W] = hi
            dl[:, R : R + W] = lo

    ROW = lax.broadcasted_iota(jnp.int32, (128, 128), 0)
    COL = lax.broadcasted_iota(jnp.int32, (128, 128), 1)

    def gram(first, second, width):
        li = pl.ds(pl.multiple_of(first * 128, 128), 128)
        ri = pl.ds(pl.multiple_of(second * 128, 128), width)

        def dot(left, right):
            return lax.dot_general(left, right, (((0,), (0,)), ((), ())), preferred_element_type=F32)

        lh, ll, rh, rlo = dh[:, li], dl[:, li], dh[:, ri], dl[:, ri]
        return dot(lh, rh) + (dot(lh, rlo) + dot(ll, rh))

    for a in range(3):
        block = gram(3 * c + a, 3 * c + a + 1, 256)
        packed[2 * a * 128 : (2 * a + 1) * 128, :] = block[:, :128]
        packed[(2 * a + 1) * 128 : (2 * a + 2) * 128, :] = block[:, 128:]

    def corner_blocks():
        @pl.when(c == 0)
        def _():
            for e in range(3):
                packed[(6 + e) * 128 : (7 + e) * 128, :] = gram(e, e + 3, 128)

        @pl.when(c == 1)
        def _():
            upper = ROW <= COL
            for e in range(3):
                packed[(6 + e) * 128 : (7 + e) * 128, :] = jnp.where(upper, gram(e, e, 128), gram(e + 3, e + 3, 128))

    pa = (x * (1 - c) + y * c, y * (1 - c) + x * c)
    pb = (pa[1], pa[0])

    def on_a(first, second, plane):
        return device(first * (1 - c) + second * c, second * (1 - c) + first * c, plane, c)

    def on_b(first, second, plane):
        return on_a(second, first, plane)

    paths = (
        (0, BA, pa, on_a, ra1, a1s, a1r, ga, ga1s, ga1r, ga2s, ga2r),
        (SPLIT, BB, pb, on_b, rb1, b1s, b1r, gb, gb1s, gb1r, gb2s, gb2r),
    )
    order = (2, 1, 3)

    first_hops = []

    def start_first(base, rows, at, on, r1, s1, t1, *_):
        size = 4 * rows
        for o in order:
            to = (at[0] + o) % 4
            src = packed.at[pl.ds(pl.multiple_of(base + to * size, 8), size)]
            first_hops.append(go(remote(src, r1.at[o - 1], s1.at[o - 1], t1.at[o - 1], on(to, at[1], z))))

    start_first(*paths[0])
    corner_blocks()
    start_first(*paths[1])
    tile[...] = jnp.zeros((8, 128), F32)
    for e in range(3):
        d = dx[:, (e + 3) * 128 : (e + 4) * 128]
        tile[e : e + 1, :] = jnp.sum(d * d, axis=0, keepdims=True)
    tiles = [go(remote(tile, rt.at[o - 1], ts.at[o - 1], tr.at[o - 1], on_a((pa[0] + o) % 4, pa[1], z))) for o in order]

    def settle(offset):
        at = chunk(offset)
        nm_ref[at] = MOMENTUM_FACTOR * mbuf[at] + s_ref[at]
        dall[at] = s_ref[at] + MOMENTUM_FACTOR * nm_ref[at]

    settle(0)
    hops["u", 0].wait_recv()
    gather_up(1)
    hops["d", 0].wait_recv()
    gather_down(1)

    pl.semaphore_wait(summed, len(around))
    for n, (base, rows, (p1, p2), on, r1, *_) in enumerate(paths):
        size = 4 * rows
        for hop in first_hops[3 * n : 3 * n + 3]:
            hop.wait_recv()
        own = pl.ds(pl.multiple_of(base + p1 * size, 8), size)
        total = (packed[own, :] + r1[0]) + (r1[1] + r1[2])
        if n == 0:
            for hop in tiles:
                hop.wait_recv()
            squares = (tile[...] + rt[0]) + (rt[1] + rt[2])
        for i in range(4):
            if n == 0:
                half[0, i, :BA] = total[i * BA : (i + 1) * BA]
                half[0, i, BA:] = squares
            else:
                half[1, i, 0:16] = total[i * BB : i * BB + 16]
                half[1, i, 16:24] = squares
                half[1, i, 24:40] = total[i * BB + 16 : (i + 1) * BB]
                half[1, i, 40:48] = squares
        for o in (2, 1, 3, 0):
            to = (p2 + o) % 4
            for h in range(2):
                plane = 2 * n + h
                copy = remote(
                    half.at[n, to, pl.ds(24 * h, 24)], rz.at[4 * o + q], ms.at[n, o, h], mr.at[o, q],
                    on(p1, to, 4 * layer + plane),
                )
                if o > 0:
                    go(copy)
                else:
                    pl.when(q != plane)(copy.start)
                    local.append((q != plane, copy))
    settle(1)
    settle(-1)
    mine_n, mine_h = q // 2, q % 2
    mine_2 = pa[1] * (1 - mine_n) + pb[1] * mine_n
    rz[q] = half[mine_n, mine_2, pl.ds(pl.multiple_of(24 * mine_h, 8), 24)]
    for o in range(4):
        for plane in range(4):
            copy = remote(piece, rz.at[4 * o + plane], ms.at[0, 0, 0], mr.at[o, plane], other)
            if o > 0:
                copy.wait_recv()
            else:
                pl.when(q != plane)(copy.wait_recv)
    sums = [rz[i] for i in range(16)]
    while len(sums) > 1:
        sums = [sums[2 * i] + sums[2 * i + 1] for i in range(len(sums) // 2)]
    at = pl.ds(pl.multiple_of(q * 24, 8), 24)
    piece[...] = sums[0]
    for o in (4, 3, 5, 2, 6, 1, 7):
        go(remote(piece, gz.at[c, at], z2s.at[o], z2r.at[c, q], device(x, y, (z + o) % NZ, layer)))

    @pl.when(layer == c)
    def _():
        gz[c, at, :] = piece[...]

    copy = remote(piece, gz.at[c, at], z2s.at[0], z2r.at[c, q], other)
    pl.when(layer != c)(copy.start)
    local.append((layer != c, copy))

    near, far = {}, {}

    def start_far(n, j):
        base, rows, (p1, p2), on, r1, s1, t1, out, u1, v1, u2, v2 = paths[n]
        block = out.at[p1, (p2 + 4 - j) % 4]
        for o in order:
            far[n, o, j] = go(remote(block, block, u2.at[o - 1, j], v2.at[o - 1, j], on((p1 + o) % 4, p2, z)))

    gathering = len(started)
    for n, (base, rows, (p1, p2), on, r1, s1, t1, out, u1, v1, u2, v2) in enumerate(paths):
        for quarter in (2 * n, 2 * n + 1):
            for h in range(2):
                arrival = remote(piece, gz.at[h, pl.ds(24 * quarter, 24)], z2s.at[0], z2r.at[h, quarter], other)
                pl.when((layer != c) | (c != h) | (q != quarter))(arrival.wait_recv)
        if n == 0:
            out[p1, p2] = gz[:, 0:BA, :]
        else:
            out[p1, p2, :, 0:16] = gz[:, 48:64, :]
            out[p1, p2, :, 16:32] = gz[:, 72:88, :]
        block = out.at[p1, p2]
        for o in order:
            near[n, o] = go(remote(block, block, u1.at[o - 1], v1.at[o - 1], on(p1, (p2 + o) % 4, z)))
    for n in range(2):
        start_far(n, 0)
    sent, started[:] = started[:gathering], started[gathering:]

    hops["u", 1].wait_recv()
    gather_up(2)
    hops["d", 1].wait_recv()
    gather_down(2)
    settle(2)
    settle(-2)

    for copy in sent:
        copy.wait_send()
    for o in order:
        for n in range(2):
            near[n, o].wait_recv()
            start_far(n, o)

    hops["u", 2].wait_recv()
    gather_up(3)
    hops["d", 2].wait_recv()
    settle(-3)
    settle(3)

    hops["u", 3].wait_recv()
    settle(-4)
    handed = go(remote(dall.at[pl.ds(4 * (1 - c), 4)], dother, dsem.at[0], dsem.at[1], other))
    for hop in far.values():
        hop.wait_recv()

    diagonals = gz[0, BA : BA + 8, :]
    trace = jnp.sum(diagonals)

    def place(i, j, block):
        g[i * 128 : (i + 1) * 128, j * 128 : (j + 1) * 128] = block

    for h in range(2):
        turned = h + c - 2 * h * c
        places = [(i * (1 - turned) + j * turned, j * (1 - turned) + i * turned) for i in range(4) for j in range(4)]
        rows_a = jnp.concatenate([ga[i, j, h] for i, j in places], axis=0)
        rows_b = jnp.concatenate([gb[i, j, h] for i, j in places], axis=0)
        for b in range(BLOCKS):
            block = rows_a[b * 128 : (b + 1) * 128] if b < 5 else rows_b[(b - 5) * 128 : (b - 4) * 128]
            if b < 6:
                i = 3 * h + b // 2
                j = (i + 1 + b % 2) % 6
            else:
                i, j = b - 6, b - 3
            if b < 6 or h == 0:
                place(i, j, block)
                place(j, i, block.T)
            else:
                trace = trace + jnp.sum(jnp.where(ROW == COL, block, 0.0))
                above = jnp.where(ROW < COL, block, 0.0)
                below = jnp.where(ROW > COL, block, 0.0)
                place(i, i, jnp.where(ROW <= COL, block, 0.0) + above.T)
                place(j, j, below + below.T + jnp.where(ROW == COL, diagonals[i : i + 1, :], 0.0))
    inverse = 1.0 / (jnp.sqrt(jnp.broadcast_to(trace, (8, 128))) + NORM_EPSILON)
    scale = inverse[0:1, 0:1]
    square = scale * scale
    for j in range(3):
        put(ah, al, slice(0, R), COLS[j], g[:, COLS[j]] * square)
    corner = lax.broadcasted_iota(jnp.int32, (256, 256), 0) == lax.broadcasted_iota(jnp.int32, (256, 256), 1)
    linear = jnp.where(corner, QUINTIC_LINEAR, 0.0)

    def polynomial(value, i, j):
        value = (QUINTIC_CUBIC * square) * g[COLS[i], COLS[j]] + QUINTIC_FIFTH * value
        return linear + value if i == j else value

    symmetric_product((ah, al), (ah, al), (ph, plo), polynomial)

    symmetric_product((ph, plo), (ah, al), (bh, bl))
    symmetric_product((ph, plo), (bh, bl), (ah, al))

    handed.wait_recv()
    factor = UPDATE_FACTOR * math.sqrt(max(D, R))
    halves = (slice(224, 448), slice(0, 224))
    every = slice(0, R)
    put(wh, wl, halves[1], every, dall[pl.ds(4 * c, 4)].reshape(224, R))
    put(wh, wl, halves[0], every, dother[...].reshape(224, R))
    for rows in halves:
        x1 = dot3((wh[rows, :], wl[rows, :]), (ph[...], plo[...])) * scale
        work[rows, :] = QUINTIC_LINEAR * x1
        put(xh, xl, rows, every, x1)
    for rows in halves:
        y1 = dot3((xh[rows, :], xl[rows, :]), (ah[...], al[...]))
        work[rows, :] = work[rows, :] + QUINTIC_CUBIC * y1
        put(wh, wl, rows, every, y1)

    def finish(rows):
        return factor * (work[rows, :] + QUINTIC_FIFTH * dot3((wh[rows, :], wl[rows, :]), (ah[...], al[...])))

    theirs[...] = finish(halves[0])
    back = go(remote(theirs, up_ref.at[c], usem.at[0], usem.at[1], other))
    up_ref[c] = finish(halves[1])
    drain()
    back.wait_recv()


def dot3(left, right):
    (lh, ll), (rh, rl) = left, right

    def dot(a, b):
        return jnp.dot(a, b, preferred_element_type=F32)

    return dot(lh, rh) + (dot(lh, rl) + dot(ll, rh))


def put(hi_ref, lo_ref, rows, cols, value):
    hi = value.astype(BF16)
    hi_ref[rows, cols] = hi
    lo_ref[rows, cols] = (value - hi.astype(F32)).astype(BF16)


COLS = [slice(j * 256, (j + 1) * 256) for j in range(3)]


def symmetric_product(left, right, out, then=None):
    (lh, ll), (rh, rl) = left, right
    for j in range(3):
        rows = slice(0, (j + 1) * 256)
        block = dot3((lh[rows, :], ll[rows, :]), (rh[:, COLS[j]], rl[:, COLS[j]]))
        for i in range(j + 1):
            value = block[COLS[i]]
            if then is not None:
                value = then(value, i, j)
            put(*out, COLS[i], COLS[j], value)
            if i < j:
                put(*out, COLS[j], COLS[i], value.T)


def update_kernel(nm_ref, up_ref, w_ref, nm_out, up_out, nw_out, nw, sems):
    copies = [pltpu.make_async_copy(nm_ref, nm_out, sems.at[0]), pltpu.make_async_copy(up_ref, up_out, sems.at[1])]
    for copy in copies:
        copy.start()
    for i in range(4):
        rows = pl.ds(i * 112, 112)
        weights = w_ref[rows, :]
        nw[rows, :] = weights - LEARNING_RATE * (up_ref[rows, :] + WEIGHT_DECAY * weights)
        copies.append(pltpu.make_async_copy(nw.at[rows], nw_out.at[rows], sems.at[2 + i]))
        copies[-1].start()
    for copy in copies:
        copy.wait()


def shards(replica_grads, momentum, weights):
    grads = pltpu.with_memory_space_constraint(replica_grads.reshape(NZ * CH, R), pltpu.HBM)
    momentum = pltpu.with_memory_space_constraint(momentum.reshape(NZ, CH, R), pltpu.HBM)
    weights = weights.reshape(NZ * CH, R)
    vmem = pl.BlockSpec(memory_space=pltpu.VMEM)
    hbm = pl.BlockSpec(memory_space=pltpu.HBM)
    sem = pltpu.SemaphoreType.DMA
    rows = pltpu.VMEM((NZ * CH, R), BF16)
    half = pltpu.VMEM((R, R), BF16)
    new_momentum, update = pl.pallas_call(
        gram_kernel,
        out_shape=(
            jax.ShapeDtypeStruct((NZ, CH, R), F32),
            jax.ShapeDtypeStruct((2, 224, R), F32),
        ),
        in_specs=[hbm, hbm],
        out_specs=(vmem, vmem),
        scratch_shapes=[
            pltpu.VMEM((NZ * CH, R), BF16),
            pltpu.VMEM((NZ, CH, R), F32),
            pltpu.VMEM((4, 4, 2, BA, 128), F32),
            pltpu.VMEM((4, 4, 2, BB, 128), F32),
            pltpu.VMEM((R, R), F32), half, half, half, half, half, half, rows, rows, rows, rows,
            pltpu.VMEM((NZ * CH, R), F32),
            pltpu.VMEM((224, R), F32),
            pltpu.VMEM((NZ, CH, R), F32),
            pltpu.VMEM((4, CH, R), F32),
            pltpu.VMEM((NZ, CH, R), F32),
            pltpu.VMEM((4, CH, R), F32),
            pltpu.VMEM((3, CH, R), F32),
            pltpu.VMEM((NZ, CH, R), F32),
            pltpu.VMEM((2 * CH, R), F32),
            pltpu.VMEM((2 * CH, R + W), BF16),
            pltpu.VMEM((2 * CH, R + W), BF16),
            pltpu.VMEM((BLOCKS * 128, 128), F32),
            pltpu.VMEM((8, 128), F32),
            pltpu.VMEM((3, 8, 128), F32),
            pltpu.VMEM((3, 4 * BA, 128), F32),
            pltpu.VMEM((3, 4 * BB, 128), F32),
            pltpu.VMEM((2, 4, 48, 128), F32),
            pltpu.VMEM((16, 24, 128), F32),
            pltpu.VMEM((24, 128), F32),
            pltpu.VMEM((2, 96, 128), F32),
            sem,
            sem,
        ]
        + [sem((4, SUB)), sem((4, SUB)), sem((3, SUB)), sem((3, SUB))]
        + [sem((4,)), sem((4,)), sem((3,)), sem((3,))]
        + [sem((SUB,))] * 2
        + [sem((3,))] * 6
        + [sem((2, 4, 2)), sem((4, 4))]
        + [sem((8,)), sem((2, 4))]
        + [sem((3,))] * 4
        + [sem((3, 4))] * 4
        + [sem((2,))] * 2
        + [pltpu.SemaphoreType.REGULAR] * 2,
        compiler_params=pltpu.CompilerParams(collective_id=0, has_side_effects=True, vmem_limit_bytes=34 << 20),
        name="gram",
    )(grads, momentum)
    like = jax.ShapeDtypeStruct((NZ * CH, R), F32)
    outs = pl.pallas_call(
        update_kernel,
        out_shape=(like, like, like),
        in_specs=[vmem] * 3,
        out_specs=(hbm, hbm, hbm),
        scratch_shapes=[pltpu.VMEM((NZ * CH, R), F32), sem((6,))],
        compiler_params=pltpu.CompilerParams(vmem_limit_bytes=4 << 20),
        name="update",
    )(new_momentum.reshape(NZ * CH, R), update.reshape(NZ * CH, R), weights)
    return tuple(o.reshape(2, 224, R) for o in outs)


def solution(mesh):
    return jax.shard_map(
        shards,
        mesh=mesh,
        in_specs=(P("dp", None, "fsdp", None), P(None, "fsdp", None), P(None, "fsdp", None)),
        out_specs=(P(None, "fsdp", None), P(None, "fsdp", None), P(None, "fsdp", None)),
        check_vma=False,
    )
```

```python
import functools
import math

import jax
import jax.numpy as jnp
from jax import lax
from jax.experimental import pallas as pl
from jax.experimental.pallas import tpu as pltpu
from jax.sharding import PartitionSpec as P

D = 7168
R = 768

QUINTIC_LINEAR = 3.4445
QUINTIC_CUBIC = -4.775
QUINTIC_FIFTH = 2.0315
MOMENTUM_FACTOR = 0.95
LEARNING_RATE = 0.02
WEIGHT_DECAY = 0.1
NORM_EPSILON = 1e-07
UPDATE_FACTOR = 0.2

MESH = pl.DeviceIdType.MESH
F32 = jnp.float32
BF16 = jnp.bfloat16
NZ = 8
CH = 56
SUB = 3
W = R // SUB
BA, BB = 40, 32
BLOCKS = 9
SPLIT = 16 * BA


def device(x, y, z, c):
    return (z, (x * 4 + y) * 2 + c)


def remote(src, dst, send, recv, target):
    return pltpu.make_async_remote_copy(
        src_ref=src, dst_ref=dst, send_sem=send, recv_sem=recv, device_id=target, device_id_type=MESH
    )


def gram_kernel(
    g_ref, m_ref, nm_ref, up_ref,
    graw, s_ref, ga, gb, g, ah, al, ph, plo, bh, bl, wh, wl, xh, xl, work, theirs, dall, dother,
    acc, rl, rs, mbuf, dx, dh, dl, packed, tile, rt, ra1, rb1, half, rz, piece, gz,
    msem, gsem, ls, lr, ss, sr, als, alr, ass, asr, cs, cr,
    a1s, a1r, b1s, b1r, ts, tr, ms, mr, z2s, z2r,
    ga1s, ga1r, gb1s, gb1r, ga2s, ga2r, gb2s, gb2r, dsem, usem, ready, summed,
):
    z = lax.axis_index("dp")
    f = lax.axis_index("fsdp")
    c = f % 2
    y = (f // 2) % 4
    x = f // 8
    layer = z // 4
    q = z % 4
    other = device(x, y, z, 1 - c)
    way = 1 - 2 * c
    up = device(x, y, (z + way + NZ) % NZ, c)
    down = device(x, y, (z - way + NZ) % NZ, c)

    def chunk(offset):
        return (z + way * offset + 2 * NZ) % NZ

    load = pltpu.make_async_copy(g_ref, graw, gsem)
    load.start()
    fetch = pltpu.make_async_copy(m_ref, mbuf, msem)
    fetch.start()

    barrier = pltpu.get_barrier_semaphore()
    greeted = [other]
    greeted += [device(x, y, (z + o) % NZ, c) for o in (1, NZ - 1)]
    beside = [device((x + o) % 4, y, z, c) for o in (1, 3)] + [device(x, (y + o) % 4, z, c) for o in (1, 3)]
    greeted += beside
    for target in greeted:
        pl.semaphore_signal(barrier, inc=1, device_id=target, device_id_type=MESH)
    load.wait()
    for i in range(4):
        rows = graw[i * 2 * CH : (i + 1) * 2 * CH, :].astype(F32)
        acc[2 * i] = rows[:CH]
        acc[2 * i + 1] = rows[CH:]
    pl.semaphore_wait(barrier, len(greeted))
    for target in beside:
        pl.semaphore_signal(ready, inc=1, device_id=target, device_id_type=MESH)

    def cols(k):
        return pl.ds(k * W, W)

    started = []
    local = []

    def go(copy):
        copy.start()
        started.append(copy)
        return copy

    def drain():
        for copy in started:
            copy.wait_send()
        for condition, copy in local:
            pl.when(condition)(copy.wait_send)
        started.clear()
        local.clear()

    def long_hop(step, k):
        return remote(acc.at[chunk(4 - step), :, cols(k)], rl.at[step, :, cols(k)], ls.at[step, k], lr.at[step, k], up)

    def short_hop(step, k):
        return remote(acc.at[chunk(step - 3), :, cols(k)], rs.at[step, :, cols(k)], ss.at[step, k], sr.at[step, k], down)

    hops = {}
    for k in range(SUB):
        hops["l", 0, k] = go(long_hop(0, k))
        hops["s", 0, k] = go(short_hop(0, k))
    for step in range(1, 4):
        for k in range(SUB):
            hops["l", step - 1, k].wait_recv()
            at = chunk(4 - step)
            acc[at, :, cols(k)] = acc[at, :, cols(k)] + rl[step - 1, :, cols(k)]
            hops["l", step, k] = go(long_hop(step, k))
            if step < 3:
                hops["s", step - 1, k].wait_recv()
                at = chunk(step - 3)
                acc[at, :, cols(k)] = acc[at, :, cols(k)] + rs[step - 1, :, cols(k)]
                hops["s", step, k] = go(short_hop(step, k))

    def gather_up(step):
        block = s_ref.at[chunk(-step)]
        hops["u", step] = go(remote(block, block, als.at[step], alr.at[step], up))

    def gather_down(step):
        block = s_ref.at[chunk(step)]
        hops["d", step] = go(remote(block, block, ass.at[step], asr.at[step], down))

    fetch.wait()
    mine = []
    for k in range(SUB):
        hops["s", 2, k].wait_recv()
        hops["l", 3, k].wait_recv()
        total = acc[z, :, cols(k)] + rs[2, :, cols(k)] + rl[3, :, cols(k)]
        s_ref[z, :, cols(k)] = total
        d = total + MOMENTUM_FACTOR * (MOMENTUM_FACTOR * mbuf[z, :, cols(k)] + total)
        dx[0:CH, cols(k)] = d
        mine.append(
            go(remote(dx.at[pl.ds(0, CH), cols(k)], dx.at[pl.ds(CH, CH), cols(k)], cs.at[k], cr.at[k], other))
        )
    gather_up(0)
    gather_down(0)

    pl.semaphore_wait(ready, len(beside))
    around = [device((x + o) % 4, y, z, c) for o in (1, 2, 3)] + [device(x, (y + o) % 4, z, c) for o in (1, 2, 3)]
    for target in around:
        pl.semaphore_signal(summed, inc=1, device_id=target, device_id_type=MESH)

    for k in range(SUB):
        mine[k].wait_recv()
        d = dx[:, cols(k)]
        hi = d.astype(BF16)
        lo = (d - hi.astype(F32)).astype(BF16)
        dh[:, cols(k)] = hi
        dl[:, cols(k)] = lo
        if k == 0:
            dh[:, R : R + W] = hi
            dl[:, R : R + W] = lo

    ROW = lax.broadcasted_iota(jnp.int32, (128, 128), 0)
    COL = lax.broadcasted_iota(jnp.int32, (128, 128), 1)

    def gram(first, second, width):
        li = pl.ds(pl.multiple_of(first * 128, 128), 128)
        ri = pl.ds(pl.multiple_of(second * 128, 128), width)

        def dot(left, right):
            return lax.dot_general(left, right, (((0,), (0,)), ((), ())), preferred_element_type=F32)

        lh, ll, rh, rlo = dh[:, li], dl[:, li], dh[:, ri], dl[:, ri]
        return dot(lh, rh) + (dot(lh, rlo) + dot(ll, rh))

    for a in range(3):
        block = gram(3 * c + a, 3 * c + a + 1, 256)
        packed[2 * a * 128 : (2 * a + 1) * 128, :] = block[:, :128]
        packed[(2 * a + 1) * 128 : (2 * a + 2) * 128, :] = block[:, 128:]

    def corner_blocks():
        @pl.when(c == 0)
        def _():
            for e in range(3):
                packed[(6 + e) * 128 : (7 + e) * 128, :] = gram(e, e + 3, 128)

        @pl.when(c == 1)
        def _():
            upper = ROW <= COL
            for e in range(3):
                packed[(6 + e) * 128 : (7 + e) * 128, :] = jnp.where(upper, gram(e, e, 128), gram(e + 3, e + 3, 128))

    pa = (x * (1 - c) + y * c, y * (1 - c) + x * c)
    pb = (pa[1], pa[0])

    def on_a(first, second, plane):
        return device(first * (1 - c) + second * c, second * (1 - c) + first * c, plane, c)

    def on_b(first, second, plane):
        return on_a(second, first, plane)

    paths = (
        (0, BA, pa, on_a, ra1, a1s, a1r, ga, ga1s, ga1r, ga2s, ga2r),
        (SPLIT, BB, pb, on_b, rb1, b1s, b1r, gb, gb1s, gb1r, gb2s, gb2r),
    )
    order = (2, 1, 3)

    first_hops = []

    def start_first(base, rows, at, on, r1, s1, t1, *_):
        size = 4 * rows
        for o in order:
            to = (at[0] + o) % 4
            src = packed.at[pl.ds(pl.multiple_of(base + to * size, 8), size)]
            first_hops.append(go(remote(src, r1.at[o - 1], s1.at[o - 1], t1.at[o - 1], on(to, at[1], z))))

    start_first(*paths[0])
    corner_blocks()
    start_first(*paths[1])
    tile[...] = jnp.zeros((8, 128), F32)
    for e in range(3):
        d = dx[:, (e + 3) * 128 : (e + 4) * 128]
        tile[e : e + 1, :] = jnp.sum(d * d, axis=0, keepdims=True)
    tiles = [go(remote(tile, rt.at[o - 1], ts.at[o - 1], tr.at[o - 1], on_a((pa[0] + o) % 4, pa[1], z))) for o in order]

    def settle(offset):
        at = chunk(offset)
        nm_ref[at] = MOMENTUM_FACTOR * mbuf[at] + s_ref[at]
        dall[at] = s_ref[at] + MOMENTUM_FACTOR * nm_ref[at]

    settle(0)
    hops["u", 0].wait_recv()
    gather_up(1)
    hops["d", 0].wait_recv()
    gather_down(1)

    pl.semaphore_wait(summed, len(around))
    for n, (base, rows, (p1, p2), on, r1, *_) in enumerate(paths):
        size = 4 * rows
        for hop in first_hops[3 * n : 3 * n + 3]:
            hop.wait_recv()
        own = pl.ds(pl.multiple_of(base + p1 * size, 8), size)
        total = (packed[own, :] + r1[0]) + (r1[1] + r1[2])
        if n == 0:
            for hop in tiles:
                hop.wait_recv()
            squares = (tile[...] + rt[0]) + (rt[1] + rt[2])
        for i in range(4):
            if n == 0:
                half[0, i, :BA] = total[i * BA : (i + 1) * BA]
                half[0, i, BA:] = squares
            else:
                half[1, i, 0:16] = total[i * BB : i * BB + 16]
                half[1, i, 16:24] = squares
                half[1, i, 24:40] = total[i * BB + 16 : (i + 1) * BB]
                half[1, i, 40:48] = squares
        for o in (2, 1, 3, 0):
            to = (p2 + o) % 4
            for h in range(2):
                plane = 2 * n + h
                copy = remote(
                    half.at[n, to, pl.ds(24 * h, 24)], rz.at[4 * o + q], ms.at[n, o, h], mr.at[o, q],
                    on(p1, to, 4 * layer + plane),
                )
                if o > 0:
                    go(copy)
                else:
                    pl.when(q != plane)(copy.start)
                    local.append((q != plane, copy))
    settle(1)
    settle(-1)
    mine_n, mine_h = q // 2, q % 2
    mine_2 = pa[1] * (1 - mine_n) + pb[1] * mine_n
    rz[q] = half[mine_n, mine_2, pl.ds(pl.multiple_of(24 * mine_h, 8), 24)]
    for o in range(4):
        for plane in range(4):
            copy = remote(piece, rz.at[4 * o + plane], ms.at[0, 0, 0], mr.at[o, plane], other)
            if o > 0:
                copy.wait_recv()
            else:
                pl.when(q != plane)(copy.wait_recv)
    sums = [rz[i] for i in range(16)]
    while len(sums) > 1:
        sums = [sums[2 * i] + sums[2 * i + 1] for i in range(len(sums) // 2)]
    at = pl.ds(pl.multiple_of(q * 24, 8), 24)
    piece[...] = sums[0]
    for o in (4, 3, 5, 2, 6, 1, 7):
        go(remote(piece, gz.at[c, at], z2s.at[o], z2r.at[c, q], device(x, y, (z + o) % NZ, layer)))

    @pl.when(layer == c)
    def _():
        gz[c, at, :] = piece[...]

    copy = remote(piece, gz.at[c, at], z2s.at[0], z2r.at[c, q], other)
    pl.when(layer != c)(copy.start)
    local.append((layer != c, copy))

    near, far = {}, {}

    def start_far(n, j):
        base, rows, (p1, p2), on, r1, s1, t1, out, u1, v1, u2, v2 = paths[n]
        block = out.at[p1, (p2 + 4 - j) % 4]
        for o in (1, 3) if j == 0 else order:
            far[n, o, j] = go(remote(block, block, u2.at[o - 1, j], v2.at[o - 1, j], on((p1 + o) % 4, p2, z)))

    def pass_on(n):
        base, rows, (p1, p2), on, r1, s1, t1, out, u1, v1, u2, v2 = paths[n]
        source = (3, 1)[n]
        far[n, source, 0].wait_recv()
        block = out.at[(p1 + 4 - source) % 4, p2]
        far[n, 2, 0] = go(remote(block, block, u2.at[1, 0], v2.at[1, 0], on((p1 + source) % 4, p2, z)))

    gathering = len(started)
    for n, (base, rows, (p1, p2), on, r1, s1, t1, out, u1, v1, u2, v2) in enumerate(paths):
        for quarter in (2 * n, 2 * n + 1):
            for h in range(2):
                arrival = remote(piece, gz.at[h, pl.ds(24 * quarter, 24)], z2s.at[0], z2r.at[h, quarter], other)
                pl.when((layer != c) | (c != h) | (q != quarter))(arrival.wait_recv)
        if n == 0:
            out[p1, p2] = gz[:, 0:BA, :]
        else:
            out[p1, p2, :, 0:16] = gz[:, 48:64, :]
            out[p1, p2, :, 16:32] = gz[:, 72:88, :]
        block = out.at[p1, p2]
        for o in order:
            near[n, o] = go(remote(block, block, u1.at[o - 1], v1.at[o - 1], on(p1, (p2 + o) % 4, z)))
    for n in range(2):
        start_far(n, 0)
    sent, started[:] = started[:gathering], started[gathering:]

    hops["u", 1].wait_recv()
    gather_up(2)
    hops["d", 1].wait_recv()
    gather_down(2)
    settle(2)
    settle(-2)

    for copy in sent:
        copy.wait_send()
    for o in order:
        for n in range(2):
            near[n, o].wait_recv()
            start_far(n, o)
    for n in range(2):
        pass_on(n)

    hops["u", 2].wait_recv()
    gather_up(3)
    hops["d", 2].wait_recv()
    settle(-3)
    settle(3)

    hops["u", 3].wait_recv()
    settle(-4)
    handed = go(remote(dall.at[pl.ds(4 * (1 - c), 4)], dother, dsem.at[0], dsem.at[1], other))
    for (n, o, j), hop in far.items():
        if j != 0 or o != (3, 1)[n]:
            hop.wait_recv()

    diagonals = gz[0, BA : BA + 8, :]
    trace = jnp.sum(diagonals)

    def place(i, j, block):
        g[i * 128 : (i + 1) * 128, j * 128 : (j + 1) * 128] = block

    for h in range(2):
        turned = h + c - 2 * h * c
        places = [(i * (1 - turned) + j * turned, j * (1 - turned) + i * turned) for i in range(4) for j in range(4)]
        rows_a = jnp.concatenate([ga[i, j, h] for i, j in places], axis=0)
        rows_b = jnp.concatenate([gb[i, j, h] for i, j in places], axis=0)
        for b in range(BLOCKS):
            block = rows_a[b * 128 : (b + 1) * 128] if b < 5 else rows_b[(b - 5) * 128 : (b - 4) * 128]
            if b < 6:
                i = 3 * h + b // 2
                j = (i + 1 + b % 2) % 6
            else:
                i, j = b - 6, b - 3
            if b < 6 or h == 0:
                place(i, j, block)
                place(j, i, block.T)
            else:
                trace = trace + jnp.sum(jnp.where(ROW == COL, block, 0.0))
                above = jnp.where(ROW < COL, block, 0.0)
                below = jnp.where(ROW > COL, block, 0.0)
                place(i, i, jnp.where(ROW <= COL, block, 0.0) + above.T)
                place(j, j, below + below.T + jnp.where(ROW == COL, diagonals[i : i + 1, :], 0.0))
    inverse = 1.0 / (jnp.sqrt(jnp.broadcast_to(trace, (8, 128))) + NORM_EPSILON)
    scale = inverse[0:1, 0:1]
    square = scale * scale
    for j in range(3):
        put(ah, al, slice(0, R), COLS[j], g[:, COLS[j]] * square)
    corner = lax.broadcasted_iota(jnp.int32, (256, 256), 0) == lax.broadcasted_iota(jnp.int32, (256, 256), 1)
    linear = jnp.where(corner, QUINTIC_LINEAR, 0.0)

    def polynomial(value, i, j):
        value = (QUINTIC_CUBIC * square) * g[COLS[i], COLS[j]] + QUINTIC_FIFTH * value
        return linear + value if i == j else value

    symmetric_product((ah, al), (ah, al), (ph, plo), polynomial)

    symmetric_product((ph, plo), (ah, al), (bh, bl))
    symmetric_product((ph, plo), (bh, bl), (ah, al))

    handed.wait_recv()
    factor = UPDATE_FACTOR * math.sqrt(max(D, R))
    halves = (slice(224, 448), slice(0, 224))
    every = slice(0, R)
    put(wh, wl, halves[1], every, dall[pl.ds(4 * c, 4)].reshape(224, R))
    put(wh, wl, halves[0], every, dother[...].reshape(224, R))
    for rows in halves:
        x1 = dot3((wh[rows, :], wl[rows, :]), (ph[...], plo[...])) * scale
        work[rows, :] = QUINTIC_LINEAR * x1
        put(xh, xl, rows, every, x1)
    for rows in halves:
        y1 = dot3((xh[rows, :], xl[rows, :]), (ah[...], al[...]))
        work[rows, :] = work[rows, :] + QUINTIC_CUBIC * y1
        put(wh, wl, rows, every, y1)

    def finish(rows):
        return factor * (work[rows, :] + QUINTIC_FIFTH * dot3((wh[rows, :], wl[rows, :]), (ah[...], al[...])))

    theirs[...] = finish(halves[0])
    back = go(remote(theirs, up_ref.at[c], usem.at[0], usem.at[1], other))
    up_ref[c] = finish(halves[1])
    drain()
    back.wait_recv()


def dot3(left, right):
    (lh, ll), (rh, rl) = left, right

    def dot(a, b):
        return jnp.dot(a, b, preferred_element_type=F32)

    return dot(lh, rh) + (dot(lh, rl) + dot(ll, rh))


def put(hi_ref, lo_ref, rows, cols, value):
    hi = value.astype(BF16)
    hi_ref[rows, cols] = hi
    lo_ref[rows, cols] = (value - hi.astype(F32)).astype(BF16)


COLS = [slice(j * 256, (j + 1) * 256) for j in range(3)]


def symmetric_product(left, right, out, then=None):
    (lh, ll), (rh, rl) = left, right
    for j in range(3):
        rows = slice(0, (j + 1) * 256)
        block = dot3((lh[rows, :], ll[rows, :]), (rh[:, COLS[j]], rl[:, COLS[j]]))
        for i in range(j + 1):
            value = block[COLS[i]]
            if then is not None:
                value = then(value, i, j)
            put(*out, COLS[i], COLS[j], value)
            if i < j:
                put(*out, COLS[j], COLS[i], value.T)


def update_kernel(nm_ref, up_ref, w_ref, nm_out, up_out, nw_out, nw, sems):
    copies = [pltpu.make_async_copy(nm_ref, nm_out, sems.at[0]), pltpu.make_async_copy(up_ref, up_out, sems.at[1])]
    for copy in copies:
        copy.start()
    for i in range(4):
        rows = pl.ds(i * 112, 112)
        weights = w_ref[rows, :]
        nw[rows, :] = weights - LEARNING_RATE * (up_ref[rows, :] + WEIGHT_DECAY * weights)
        copies.append(pltpu.make_async_copy(nw.at[rows], nw_out.at[rows], sems.at[2 + i]))
        copies[-1].start()
    for copy in copies:
        copy.wait()


def shards(replica_grads, momentum, weights):
    grads = pltpu.with_memory_space_constraint(replica_grads.reshape(NZ * CH, R), pltpu.HBM)
    momentum = pltpu.with_memory_space_constraint(momentum.reshape(NZ, CH, R), pltpu.HBM)
    weights = weights.reshape(NZ * CH, R)
    vmem = pl.BlockSpec(memory_space=pltpu.VMEM)
    hbm = pl.BlockSpec(memory_space=pltpu.HBM)
    sem = pltpu.SemaphoreType.DMA
    rows = pltpu.VMEM((NZ * CH, R), BF16)
    half = pltpu.VMEM((R, R), BF16)
    new_momentum, update = pl.pallas_call(
        gram_kernel,
        out_shape=(
            jax.ShapeDtypeStruct((NZ, CH, R), F32),
            jax.ShapeDtypeStruct((2, 224, R), F32),
        ),
        in_specs=[hbm, hbm],
        out_specs=(vmem, vmem),
        scratch_shapes=[
            pltpu.VMEM((NZ * CH, R), BF16),
            pltpu.VMEM((NZ, CH, R), F32),
            pltpu.VMEM((4, 4, 2, BA, 128), F32),
            pltpu.VMEM((4, 4, 2, BB, 128), F32),
            pltpu.VMEM((R, R), F32), half, half, half, half, half, half, rows, rows, rows, rows,
            pltpu.VMEM((NZ * CH, R), F32),
            pltpu.VMEM((224, R), F32),
            pltpu.VMEM((NZ, CH, R), F32),
            pltpu.VMEM((4, CH, R), F32),
            pltpu.VMEM((NZ, CH, R), F32),
            pltpu.VMEM((4, CH, R), F32),
            pltpu.VMEM((3, CH, R), F32),
            pltpu.VMEM((NZ, CH, R), F32),
            pltpu.VMEM((2 * CH, R), F32),
            pltpu.VMEM((2 * CH, R + W), BF16),
            pltpu.VMEM((2 * CH, R + W), BF16),
            pltpu.VMEM((BLOCKS * 128, 128), F32),
            pltpu.VMEM((8, 128), F32),
            pltpu.VMEM((3, 8, 128), F32),
            pltpu.VMEM((3, 4 * BA, 128), F32),
            pltpu.VMEM((3, 4 * BB, 128), F32),
            pltpu.VMEM((2, 4, 48, 128), F32),
            pltpu.VMEM((16, 24, 128), F32),
            pltpu.VMEM((24, 128), F32),
            pltpu.VMEM((2, 96, 128), F32),
            sem,
            sem,
        ]
        + [sem((4, SUB)), sem((4, SUB)), sem((3, SUB)), sem((3, SUB))]
        + [sem((4,)), sem((4,)), sem((3,)), sem((3,))]
        + [sem((SUB,))] * 2
        + [sem((3,))] * 6
        + [sem((2, 4, 2)), sem((4, 4))]
        + [sem((8,)), sem((2, 4))]
        + [sem((3,))] * 4
        + [sem((3, 4))] * 4
        + [sem((2,))] * 2
        + [pltpu.SemaphoreType.REGULAR] * 2,
        compiler_params=pltpu.CompilerParams(collective_id=0, has_side_effects=True, vmem_limit_bytes=34 << 20),
        name="gram",
    )(grads, momentum)
    like = jax.ShapeDtypeStruct((NZ * CH, R), F32)
    outs = pl.pallas_call(
        update_kernel,
        out_shape=(like, like, like),
        in_specs=[vmem] * 3,
        out_specs=(hbm, hbm, hbm),
        scratch_shapes=[pltpu.VMEM((NZ * CH, R), F32), sem((6,))],
        compiler_params=pltpu.CompilerParams(vmem_limit_bytes=4 << 20),
        name="update",
    )(new_momentum.reshape(NZ * CH, R), update.reshape(NZ * CH, R), weights)
    return tuple(o.reshape(2, 224, R) for o in outs)


def solution(mesh):
    return jax.shard_map(
        shards,
        mesh=mesh,
        in_specs=(P("dp", None, "fsdp", None), P(None, "fsdp", None), P(None, "fsdp", None)),
        out_specs=(P(None, "fsdp", None), P(None, "fsdp", None), P(None, "fsdp", None)),
        check_vma=False,
    )
```
